128 devices in a mesh: row: 16 (over y, x_hi, core), col: 8 (over z, x_lo).
Axes of the slice: x: 4 (x_hi: 2, x_lo: 2; x = x_hi * 2 + x_lo), y: 4, z: 4, core: 2. Of those that a mesh axis runs over, the one named last changes fastest.
Arguments:
- cotangent: bfloat16 [512, 512, 128], P('row', 'col'), may hold values from -6 to 6
- activations: bfloat16 [3, 512, 512, 128], P(None, 'row', 'col'), may hold values from 0 to 2
- active_masks: int32 [3, 512, 512, 128], P(None, 'row', 'col'), may hold values 0 or 1
- weights: bfloat16 [3, 9, 128, 128], replicated, may hold values from -0.1875 to 0.1875
Outputs:
- data_gradient: bfloat16 [512, 512, 128], P('row', 'col')
- weight_gradients: float32 [3, 9, 128, 128], replicated
The draws below stay inside these ranges and needn't reach their ends.
All inputs are finite; a program needn't handle non-finite values. No bound on the sum of `active_masks` on one device may be relied on, other than what follows from the above.
Results may differ from the reference program's by a relative error of at most 0.0054.
Values may be sent and summed in bfloat16 or wider, within the bound.
No kernel may reach another device: no remote copies, remote signals or barrier semaphores. Data moves between devices by JAX's collectives and lax.ppermute only.
A program may use at most 64 MiB of HBM per device.

```python
import jax
import jax.numpy as jnp

C = 128
BLOCKS = 3
N = 512


def plant(drawn, own_key, low, top_value):
    extent = drawn.shape
    place = [jax.random.randint(jax.random.fold_in(own_key, axis), (), 0, extent[axis]) for axis in range(len(extent))]
    drawn = drawn.at[tuple(place)].set(low)
    longest = extent.index(max(extent))
    place[longest] = (place[longest] + 1) % extent[longest]
    return drawn.at[tuple(place)].set(top_value)


def shard_levels(rng, extent, pieces, smallest, top_value):
    def one(position, blocks):
        heights = jax.random.uniform(jax.random.fold_in(jax.random.fold_in(rng, 6), position), (blocks,), jnp.float32, smallest / len(pieces), top_value / len(pieces))
        return jnp.repeat(jnp.exp(heights), extent[position] // blocks).reshape((-1,) + (1,) * (len(extent) - position - 1))

    gain = one(*pieces[0])
    for cut in pieces[1:]:
        gain = gain * one(*cut)
    return gain


def scatter_about(own_key, extent, spread, most, pieces=(), kind=jnp.bfloat16):
    gain = shard_levels(own_key, extent, pieces, -0.22, 0.18) if pieces else 1.0
    entries = jax.random.normal(own_key, extent, jnp.float32) * spread * gain
    return jnp.minimum(jnp.maximum(entries, -most), most).astype(kind)


def setup_inputs(seed: int = 0) -> dict:
    streams_of = jax.random.split(jax.random.key(seed), 5)
    cotangent = scatter_about(streams_of[0], (N, N, C), 1.0, 6.0, ((0, 16), (1, 8)))
    activations = jnp.clip(2.0 * jax.random.uniform(streams_of[1], (BLOCKS, N, N, C), jnp.float32) ** shard_levels(streams_of[1], (BLOCKS, N, N, C), ((1, 16), (2, 8)), -0.2, 0.2), 0.0, 2.0).astype(jnp.bfloat16)
    active_masks = plant((jax.random.randint(streams_of[2], (BLOCKS, N, N, C), 0, 2) < 1).astype(jnp.int32), jax.random.fold_in(streams_of[2], 1), 0, 1)
    weights = scatter_about(streams_of[3], (BLOCKS, 9, C, C), (9 * C) ** -0.5, 0.1875)
    return dict(cotangent=cotangent, activations=activations, active_masks=active_masks, weights=weights)


def reference(cotangent, activations, active_masks, weights):
    gradient = cotangent
    results = []
    for layer_index in reversed(range(BLOCKS)):
        dilation = 2 ** layer_index
        mask_now = active_masks[layer_index] > 0
        inputs_now = jnp.where(mask_now, activations[layer_index], jnp.zeros_like(activations[layer_index]))
        wide = gradient.astype(jnp.float32)
        symmetric = ((wide + jnp.transpose(wide, (1, 0, 2))) * 0.5).astype(jnp.bfloat16)
        padded = jnp.pad(symmetric, ((dilation, dilation), (dilation, dilation), (0, 0)))
        flat_inputs = inputs_now.reshape(-1, C)
        accumulated = jnp.zeros((N * N, C), jnp.float32)
        kernel_terms = []
        for tap_down in range(3):
            for tap_across in range(3):
                tap_index = 3 * tap_down + tap_across
                start_down = dilation * (2 - tap_down)
                start_across = dilation * (2 - tap_across)
                shifted = padded[start_down:start_down + N, start_across:start_across + N]
                flat_shift = shifted.reshape(-1, C)
                weight_term = jnp.dot(flat_inputs.T, flat_shift, preferred_element_type=jnp.float32) / N
                kernel_terms.append(weight_term)
                accumulated = accumulated + jnp.dot(flat_shift, weights[layer_index, tap_index].T, preferred_element_type=jnp.float32)
        results.append(jnp.stack(kernel_terms))
        input_change = accumulated.reshape(N, N, C)
        gradient = (gradient.astype(jnp.float32) + jnp.where(mask_now, input_change, jnp.float32(0.0))).astype(jnp.bfloat16)
    weight_gradients = jnp.stack(results[::-1])
    return gradient, weight_gradients
```

```python
import numpy as np
import jax
import jax.numpy as jnp
from jax import lax
from jax.sharding import Mesh, PartitionSpec as P

NAMES = ("y", "xh", "core", "z", "xl")
SIZES = (4, 2, 2, 4, 2)
CHIPS = ("y", "xh", "z", "xl")
BF = jnp.bfloat16
F32 = jnp.float32


def index_grid():
    return np.arange(128).reshape(SIZES)


def neighbour(down, across):
    pairs = []
    for r in range(16):
        for c in range(8):
            if 0 <= r + down < 16 and 0 <= c + across < 8:
                pairs.append((r * 8 + c, (r + down) * 8 + c + across))
    return pairs


def mirror_steps(part):
    grid = index_grid()
    first, second = [], []
    step = 1 if part == 0 else -1
    for y, xh, c, z, xl in np.ndindex(*SIZES):
        core = c if part == 0 else 1 - c
        source = int(grid[y, xh, c, z, xl])
        if (z - y) % 4 == 2:
            middle = int(grid[(y + step) % 4, xh, c, (z + step) % 4, xl])
            first.append((source, middle))
            second.append((middle, int(grid[(y + 2 * step) % 4, xl, core, (z + 2 * step) % 4, xh])))
        else:
            first.append((source, int(grid[z, xl, core, y, xh])))
    return first, second


def shift(x, pairs):
    return lax.ppermute(x, NAMES, pairs)


def halo(x, width, dim):
    rank = x.ndim
    low = neighbour(1, 0) if dim == rank - 3 else neighbour(0, 1)
    high = neighbour(-1, 0) if dim == rank - 3 else neighbour(0, -1)
    size = x.shape[dim]
    before = shift(lax.slice_in_dim(x, size - width, size, axis=dim), low)
    after = shift(lax.slice_in_dim(x, 0, width, axis=dim), high)
    return jnp.concatenate([before, x, after], axis=dim)


def halos(x, width):
    x = halo(x, width, x.ndim - 3)
    return halo(x, width, x.ndim - 2)


def mirrored(x, margin):
    core = lax.axis_index("core")
    rows, cols = x.shape[-3] - 2 * margin, x.shape[-2] - 2 * margin
    half = cols // 2
    got = []
    for part in (0, 1):
        which = core if part == 0 else 1 - core
        piece = lax.dynamic_slice_in_dim(x, margin * core, rows + margin, axis=x.ndim - 3)
        piece = lax.dynamic_slice_in_dim(piece, half * which, half + 2 * margin, axis=x.ndim - 2)
        first, second = mirror_steps(part)
        direct = shift(piece, first)
        relayed = shift(direct, second)
        got.append((direct, relayed))
    far = ((lax.axis_index("z") - lax.axis_index("y")) % 4) == 2
    got = [jnp.swapaxes(jnp.where(far, r, d), -3, -2) for d, r in got]
    left = jnp.where(core == 0, got[0], got[1])
    right = jnp.where(core == 0, got[1], got[0])
    return jnp.concatenate([left, right], axis=-2)


def total(x):
    core = lax.axis_index("core")
    rows = x.shape[0] // 2
    x = x.reshape(2, rows, 128)
    keep = lax.dynamic_index_in_dim(x, core, 0, False)
    send = lax.dynamic_index_in_dim(x, 1 - core, 0, False).astype(BF)
    grid = index_grid()
    swap = [(int(grid[y, a, c, z, b]), int(grid[y, a, 1 - c, z, b])) for y, a, c, z, b in np.ndindex(*SIZES)]
    part = (keep + shift(send, swap).astype(F32)).astype(BF).reshape(64, rows // 64, 128)
    terms = lax.all_to_all(part, CHIPS, 0, 0, tiled=True)
    mine = jnp.sum(terms.astype(F32), axis=0).astype(BF)
    copies = jnp.broadcast_to(mine[None], terms.shape)
    whole = lax.all_to_all(copies, CHIPS, 0, 0, tiled=True).reshape(rows, 128)
    other = shift(whole, swap)
    low = jnp.where(core == 0, whole, other)
    high = jnp.where(core == 0, other, whole)
    return jnp.concatenate([low, high], axis=0).astype(F32)


def conv(sym, kernel, dilation):
    return lax.conv_general_dilated(
        sym[None], kernel, (1, 1), "VALID", rhs_dilation=(dilation, dilation),
        dimension_numbers=("NHWC", "HWIO", "NHWC"), preferred_element_type=F32,
    )[0]


def taps(sym, height, extent, dilation):
    pieces = []
    for a in range(3):
        for b in range(3):
            u, v = dilation * (2 - a), dilation * (2 - b)
            pieces.append(sym[u : u + height, v : v + extent])
    return jnp.stack(pieces, axis=2)


def middle(x, margin):
    return x[margin : x.shape[0] - margin, margin : x.shape[1] - margin]


def per_device(cotangent, activations, active_masks, weights):
    height, extent, channels = cotangent.shape
    side = height * 16
    inputs = jnp.where(active_masks > 0, activations, jnp.zeros_like(activations))
    flip = mirrored(cotangent, 0)
    wide = cotangent.astype(F32)
    sym = ((wide + flip.astype(F32)) * 0.5).astype(BF)
    own = halos((active_masks[1:] > 0).astype(BF), 3)
    sym = halos(sym, 7)
    turned = mirrored(own, 3)

    kernels = weights.reshape(3, 3, 3, channels, channels)[:, ::-1, ::-1].transpose(0, 1, 2, 4, 3)
    both = jnp.concatenate([kernels, kernels.transpose(0, 2, 1, 3, 4)], axis=-1)
    gradient = wide
    collected = []
    for layer, margin in ((2, 3), (1, 1), (0, 0)):
        dilation = 2**layer
        stacked = taps(middle(sym, margin), height, extent, dilation) if margin else taps(sym, height, extent, dilation)
        collected.append(
            jnp.einsum("yxi,yxko->kio", inputs[layer], stacked, preferred_element_type=F32) / side
        )
        if layer:
            change = conv(sym, both[layer], dilation)
            crop = 3 - margin
            ahead = middle(own[layer - 1], crop).astype(F32) * change[..., :channels]
            back = middle(turned[layer - 1], crop).astype(F32) * change[..., channels:]
            gradient = gradient + middle(ahead, margin)
            sym = (middle(sym, dilation).astype(F32) + 0.5 * (ahead + back)).astype(BF)
        else:
            change = conv(sym, kernels[0], 1)
            gradient = gradient + jnp.where(active_masks[0] > 0, change, 0.0)
    terms = jnp.stack(collected[::-1])
    return gradient.astype(BF), total(terms.reshape(-1, channels)).reshape(terms.shape)


def solution(mesh):
    fine = Mesh(mesh.devices.reshape(SIZES), NAMES)
    rows, cols = ("y", "xh", "core"), ("z", "xl")
    in_specs = (P(rows, cols, None), P(None, rows, cols, None), P(None, rows, cols, None), P())
    out_specs = (P(rows, cols, None), P())
    return jax.shard_map(per_device, mesh=fine, in_specs=in_specs, out_specs=out_specs, check_vma=False)
```

```python
import numpy as np
import jax
import jax.numpy as jnp
from jax import lax
from jax.experimental import pallas as pl
from jax.experimental.pallas import tpu as pltpu
from jax.sharding import Mesh, PartitionSpec as P

NAMES = ("y", "xh", "core", "z", "xl")
SIZES = (4, 2, 2, 4, 2)
CHIPS = ("y", "xh", "z", "xl")
BF = jnp.bfloat16
F32 = jnp.float32


def index_grid():
    return np.arange(128).reshape(SIZES)


def neighbour(down, across):
    pairs = []
    for r in range(16):
        for c in range(8):
            if 0 <= r + down < 16 and 0 <= c + across < 8:
                pairs.append((r * 8 + c, (r + down) * 8 + c + across))
    return pairs


def mirror_steps():
    grid = index_grid()
    first, second = [], []
    for y, xh, c, z, xl in np.ndindex(*SIZES):
        source = int(grid[y, xh, c, z, xl])
        target = int(grid[z, xl, c, y, xh])
        if (z - y) % 4 == 2:
            step = 1 if c == 0 else -1
            relay = ((y + step) % 4, xl, c, (z + step) % 4, xh) if c == 0 else ((y + step) % 4, xh, c, (z + step) % 4, xl)
            first.append((source, int(grid[relay])))
            second.append((int(grid[relay]), target))
        else:
            first.append((source, target))
    return first, second


def core_swap():
    grid = index_grid()
    return [
        (int(grid[y, a, c, z, b]), int(grid[y, a, 1 - c, z, b]))
        for y, a, c, z, b in np.ndindex(*SIZES)
    ]


def shift(x, pairs):
    return lax.ppermute(x, NAMES, pairs)


WIDTHS = (7, 1, 3, 1, 3)
STARTS = (0, 7, 8, 11, 12)
VMEM = 50 * 2**20


def roll8(x, by):
    by = by % 8
    return pltpu.roll(x, by, 1) if by else x


def pack_kernel(sym_ref, own_ref, turned_ref, low_ref, high_ref, right_ref, left_ref, edges):
    edges[...] = jnp.zeros_like(edges)
    tiles = (sym_ref, own_ref.at[0], own_ref.at[1], turned_ref.at[0], turned_ref.at[1])
    for k, (tile, w, at) in enumerate(zip(tiles, WIDTHS, STARTS)):
        for side, cols in ((0, slice(48, 64)), (1, slice(0, 16))):
            for rows, part in (
                (slice(8 - w, 8), low_ref[at : at + w, cols]),
                (slice(8, 40), tile[:, cols]),
                (slice(40, 40 + w), high_ref[at : at + w, cols]),
            ):
                wide = part.astype(F32)
                edges[side, k, rows] = wide[:, 8:] if side == 0 else wide[:, :8]
    place = lax.broadcasted_iota(jnp.int32, (48, 8, 128), 1)
    for side, out, moves in ((0, right_ref, (1, 4, 5, 0)), (1, left_ref, (0, 1, 4, 5))):
        one = [roll8(edges[side, 1 + k], by) for k, by in enumerate(moves)]
        block = jnp.where(place == 0, one[0], jnp.where(place < 4, one[1], jnp.where(place == 4, one[2], one[3])))
        out[...] = jnp.concatenate([edges[side, 0], block], axis=1).astype(BF)


def pack(sym, own, turned, low, high):
    shape = jax.ShapeDtypeStruct((48, 16, 128), BF)
    return pl.pallas_call(
        pack_kernel,
        out_shape=(shape, shape),
        scratch_shapes=[pltpu.VMEM((2, 5, 48, 8, 128), F32)],
        compiler_params=pltpu.CompilerParams(vmem_limit_bytes=VMEM),
        name="pack",
    )(sym, own, turned, low, high)


def blocks_kernel(
    sym_ref, own_ref, turned_ref, low_ref, high_ref, left_ref, right_ref, inputs_ref, weights_ref,
    terms_ref, last_ref, ahead_ref, sym, masks, patches, change,
):
    sym[0:1] = jnp.zeros((1, 96, 128), F32)
    sym[47:48] = jnp.zeros((1, 96, 128), F32)
    sym[8:40, 8:72] = sym_ref[...].astype(F32)
    sym[1:8, 8:72] = low_ref[0:7].astype(F32)
    sym[40:47, 8:72] = high_ref[0:7].astype(F32)
    before, after = left_ref[...].astype(F32), right_ref[...].astype(F32)
    sym[:, 80:88] = before[:, :8]
    sym[:, 72:80] = after[:, :8]
    masks[:, 4:8] = jnp.zeros((4, 4, 80, 128), F32)
    masks[:, 40:44] = jnp.zeros((4, 4, 80, 128), F32)
    tiles = (own_ref.at[0], own_ref.at[1], turned_ref.at[0], turned_ref.at[1])
    for k, (lows, highs) in enumerate(((7, 0), (4, 7), (3, 4), (0, 3))):
        w, at = WIDTHS[k + 1], STARTS[k + 1]
        masks[k, 8:40, 0:64] = tiles[k][...].astype(F32)
        masks[k, 8 - w : 8, 0:64] = low_ref[at : at + w].astype(F32)
        masks[k, 40 : 40 + w, 0:64] = high_ref[at : at + w].astype(F32)
        masks[k, :, 72:80] = roll8(before[:, 8:], lows)
        masks[k, :, 64:72] = roll8(after[:, 8:], highs)

    for layer in (2, 1, 0):
        d = 2**layer
        first, count = ((8, 32), (6, 36), (4, 40))[layer]
        sym[:, 0:8] = sym[:, 80:88]
        sym[:, 88:96] = sym[:, 8:16]
        if layer:
            def gather(f, carry):
                for v in range(3):
                    patches[f, :, v * 128 : (v + 1) * 128] = sym[f, 8 + d * (v - 1) : 88 + d * (v - 1)].astype(BF)
                return carry

            lax.fori_loop(first - d, first + count + d, gather, 0, unroll=2)
            source, base = patches, 8
        else:
            def gather(f, carry):
                for v in range(3):
                    last_ref[f - 7, :, v * 128 : (v + 1) * 128] = sym[f, 7 + v : 71 + v].astype(BF)
                return carry

            lax.fori_loop(7, 41, gather, 0, unroll=2)
            source, base = last_ref, 1

        total = None
        for r in (0, 16):
            right = jnp.concatenate(
                [
                    source[base + r + d * (u - 1) : base + r + 16 + d * (u - 1), 0:64].reshape(1024, 384)
                    for u in range(3)
                ],
                axis=1,
            )
            term = jnp.dot(inputs_ref[layer, :, r * 64 : (r + 16) * 64], right, preferred_element_type=F32)
            total = term if total is None else total + term
        for t in range(9):
            terms_ref[layer, 8 - t] = total[:, t * 128 : (t + 1) * 128] * (1.0 / 512.0)
        if layer:
            def step(i, carry):
                f = first + 4 * i
                rows = jnp.concatenate(
                    [patches[pl.ds(f + d * (u - 1), 4)].reshape(320, 384) for u in range(3)], axis=1
                )
                out = jnp.dot(rows, weights_ref[layer], preferred_element_type=F32)
                ahead = masks[layer - 1, pl.ds(f, 4)] * out[:, :128].reshape(4, 80, 128)
                back = masks[layer + 1, pl.ds(f, 4)] * out[:, 128:].reshape(4, 80, 128)
                sym[pl.ds(f, 4), 8:88] = sym[pl.ds(f, 4), 8:88] + 0.5 * (ahead + back)
                if layer == 2:
                    change[pl.ds(f, 4)] = ahead[:, :64]
                else:
                    change[pl.ds(f, 4)] = change[pl.ds(f, 4)] + ahead[:, :64]
                return carry

            lax.fori_loop(0, count // 4, step, 0)
    ahead_ref[...] = change[8:40]


def blocks(sym, own, turned, low, high, left, right, inputs, weights):
    return pl.pallas_call(
        blocks_kernel,
        out_shape=(
            jax.ShapeDtypeStruct((3, 9, 128, 128), F32),
            jax.ShapeDtypeStruct((34, 64, 384), BF),
            jax.ShapeDtypeStruct((32, 64, 128), F32),
        ),
        scratch_shapes=[
            pltpu.VMEM((48, 96, 128), F32),
            pltpu.VMEM((4, 48, 80, 128), F32),
            pltpu.VMEM((48, 80, 384), BF),
            pltpu.VMEM((48, 64, 128), F32),
        ],
        compiler_params=pltpu.CompilerParams(vmem_limit_bytes=VMEM),
        cost_estimate=pl.CostEstimate(flops=8 * 10**9, bytes_accessed=2 * 10**7, transcendentals=0),
        name="blocks",
    )(sym, own, turned, low, high, left, right, inputs, weights)


def last_kernel(patches_ref, weights_ref, mask_ref, cotangent_ref, ahead_ref, out_ref):
    def step(i, carry):
        f = 8 * i
        rows = jnp.concatenate([patches_ref[pl.ds(f + u, 8)].reshape(512, 384) for u in range(3)], axis=1)
        change = jnp.dot(rows, weights_ref[...], preferred_element_type=F32).reshape(8, 64, 128)
        here = pl.ds(f, 8)
        wide = cotangent_ref[here].astype(F32) + ahead_ref[here]
        out_ref[here] = (wide + jnp.where(mask_ref[here] > 0, change, 0.0)).astype(BF)
        return carry

    lax.fori_loop(0, 4, step, 0)


def last(patches, weights, mask, cotangent, ahead):
    return pl.pallas_call(
        last_kernel,
        out_shape=jax.ShapeDtypeStruct((32, 64, 128), BF),
        compiler_params=pltpu.CompilerParams(vmem_limit_bytes=VMEM),
        cost_estimate=pl.CostEstimate(flops=6 * 10**8, bytes_accessed=5 * 10**6, transcendentals=0),
        name="last",
    )(patches, weights, mask, cotangent, ahead)


def mirrored(x):
    core = lax.axis_index("core")
    half = x.shape[2] // 2
    keep = lax.dynamic_slice_in_dim(x, half * core, half, axis=2)
    send = lax.dynamic_slice_in_dim(x, half * (1 - core), half, axis=2)
    got = shift(send, core_swap())
    low = jnp.where(core == 0, keep, got)
    high = jnp.where(core == 0, got, keep)
    piece = jnp.concatenate([low, high], axis=1)
    first, second = mirror_steps()
    direct = shift(piece, first)
    relayed = shift(direct, second)
    far = ((lax.axis_index("z") - lax.axis_index("y")) % 4) == 2
    return jnp.swapaxes(jnp.where(far, relayed, direct), 1, 2)


def total(x):
    core = lax.axis_index("core")
    rows = x.shape[0] // 2
    x = x.reshape(2, rows, 128)
    keep = lax.dynamic_index_in_dim(x, core, 0, False)
    send = lax.dynamic_index_in_dim(x, 1 - core, 0, False).astype(BF)
    swap = core_swap()
    part = (keep + shift(send, swap).astype(F32)).astype(BF).reshape(64, rows // 64, 128)
    terms = lax.all_to_all(part, CHIPS, 0, 0, tiled=True)
    mine = jnp.sum(terms.astype(F32), axis=0).astype(BF)
    copies = jnp.broadcast_to(mine[None], terms.shape)
    whole = lax.all_to_all(copies, CHIPS, 0, 0, tiled=True).reshape(rows, 128)
    other = shift(whole, swap)
    low = jnp.where(core == 0, whole, other)
    high = jnp.where(core == 0, other, whole)
    return jnp.concatenate([low, high], axis=0).astype(F32)


def per_device(cotangent, activations, active_masks, weights):
    channels = cotangent.shape[-1]
    own = (active_masks[1:] > 0).astype(BF)
    flip = mirrored(jnp.concatenate([cotangent[None], own], axis=0))
    sym = ((cotangent.astype(F32) + flip[0].astype(F32)) * 0.5).astype(BF)
    turned = flip[1:]
    parts = [sym, own[0], own[1], turned[0], turned[1]]
    low = shift(jnp.concatenate([p[32 - w :] for p, w in zip(parts, WIDTHS)]), neighbour(1, 0))
    high = shift(jnp.concatenate([p[:w] for p, w in zip(parts, WIDTHS)]), neighbour(-1, 0))
    ends, starts = pack(sym, own, turned, low, high)
    left = shift(ends, neighbour(0, 1))
    right = shift(starts, neighbour(0, -1))

    inputs = jnp.where(active_masks > 0, activations, jnp.zeros_like(activations))
    inputs = inputs.reshape(3, -1, channels).swapaxes(1, 2)
    kernels = weights.reshape(3, 3, 3, channels, channels)[:, ::-1, ::-1].swapaxes(3, 4)
    both = jnp.concatenate([kernels, kernels.swapaxes(1, 2)], axis=-1).reshape(3, -1, 2 * channels)
    terms, patches, ahead = blocks(sym, own, turned, low, high, left, right, inputs, both)
    gradient = last(patches, kernels[0].reshape(-1, channels), active_masks[0], cotangent, ahead)
    return gradient, total(terms.reshape(-1, channels)).reshape(terms.shape)


def solution(mesh):
    fine = Mesh(mesh.devices.reshape(SIZES), NAMES)
    rows, cols = ("y", "xh", "core"), ("z", "xl")
    in_specs = (P(rows, cols, None), P(None, rows, cols, None), P(None, rows, cols, None), P())
    out_specs = (P(rows, cols, None), P())
    return jax.shard_map(per_device, mesh=fine, in_specs=in_specs, out_specs=out_specs, check_vma=False)
```

```python
import numpy as np
import jax
import jax.numpy as jnp
from jax import lax
from jax.experimental import pallas as pl
from jax.experimental.layout import Layout, with_layout_constraint
from jax.experimental.pallas import tpu as pltpu
from jax.sharding import Mesh, PartitionSpec as P

NAMES = ("y", "xh", "core", "z", "xl")
SIZES = (4, 2, 2, 4, 2)
CHIPS = ("y", "xh", "z", "xl")
BF = jnp.bfloat16
F32 = jnp.float32


def index_grid():
    return np.arange(128).reshape(SIZES)


def neighbour(down, across):
    pairs = []
    for r in range(16):
        for c in range(8):
            if 0 <= r + down < 16 and 0 <= c + across < 8:
                pairs.append((r * 8 + c, (r + down) * 8 + c + across))
    return pairs


def mirror_steps():
    grid = index_grid()
    first, second = [], []
    for y, xh, c, z, xl in np.ndindex(*SIZES):
        source = int(grid[y, xh, c, z, xl])
        target = int(grid[z, xl, c, y, xh])
        if (z - y) % 4 == 2:
            step = 1 if c == 0 else -1
            relay = ((y + step) % 4, xl, c, (z + step) % 4, xh) if c == 0 else ((y + step) % 4, xh, c, (z + step) % 4, xl)
            first.append((source, int(grid[relay])))
            second.append((int(grid[relay]), target))
        else:
            first.append((source, target))
    return first, second


def core_swap():
    grid = index_grid()
    return [
        (int(grid[y, a, c, z, b]), int(grid[y, a, 1 - c, z, b]))
        for y, a, c, z, b in np.ndindex(*SIZES)
    ]


def shift(x, pairs):
    return lax.ppermute(x, NAMES, pairs)


WIDTHS = (7, 1, 3, 1, 3)
STARTS = (0, 7, 8, 11, 12)
STEPS = (32, 18, 20)


def roll8(x, by):
    by = by % 8
    return pltpu.roll(x, by, 1) if by else x


def call(body, name, out_shape, *args, scratch=(), flops=10**6, moved=10**6, room=8, far=0):
    return pl.pallas_call(
        body,
        out_shape=out_shape,
        in_specs=[pl.BlockSpec(memory_space=pltpu.VMEM)] * (len(args) - far) + [pl.BlockSpec(memory_space=pltpu.HBM)] * far,
        scratch_shapes=list(scratch),
        compiler_params=pltpu.CompilerParams(vmem_limit_bytes=room * 2**20),
        cost_estimate=pl.CostEstimate(flops=flops, bytes_accessed=moved, transcendentals=0),
        name=name,
    )(*args)


def symmetric_kernel(cotangent_ref, flip_ref, own_ref, sym_ref, down_ref, up_ref):
    wide = cotangent_ref[...].astype(F32) + flip_ref[0].astype(F32)
    sym_ref[...] = (wide * 0.5).astype(BF)
    tiles = (sym_ref, own_ref.at[0], own_ref.at[1], flip_ref.at[1], flip_ref.at[2])
    for tile, w, at in zip(tiles, WIDTHS, STARTS):
        down_ref[at : at + w] = tile[32 - w : 32]
        up_ref[at : at + w] = tile[0:w]


def pack_kernel(sym_ref, own_ref, flip_ref, low_ref, high_ref, ends_ref, starts_ref, edges):
    edges[...] = jnp.zeros_like(edges)
    tiles = (sym_ref, own_ref.at[0], own_ref.at[1], flip_ref.at[1], flip_ref.at[2])
    for k, (tile, w, at) in enumerate(zip(tiles, WIDTHS, STARTS)):
        for side, cols in ((0, slice(48, 64)), (1, slice(0, 16))):
            for rows, part in (
                (slice(8 - w, 8), low_ref[at : at + w, cols]),
                (slice(8, 40), tile[:, cols]),
                (slice(40, 40 + w), high_ref[at : at + w, cols]),
            ):
                wide = part.astype(F32)
                edges[side, k, rows] = wide[:, 8:] if side == 0 else wide[:, :8]
    place = lax.broadcasted_iota(jnp.int32, (48, 8, 128), 1)
    for side, out, moves in ((0, ends_ref, (1, 4, 5, 0)), (1, starts_ref, (0, 1, 4, 5))):
        one = [roll8(edges[side, 1 + k], by) for k, by in enumerate(moves)]
        block = jnp.where(place == 0, one[0], jnp.where(place < 4, one[1], jnp.where(place == 4, one[2], one[3])))
        out[...] = jnp.concatenate([edges[side, 0], block], axis=1).astype(BF)


def blocks_kernel(
    sym_ref, own_ref, flip_ref, low_ref, high_ref, left_ref, right_ref,
    cotangent_hbm, mask_hbm, inputs_hbm, weights_hbm, gradient_ref, terms_ref,
    sym, masks, patches, change, cotangent_ref, mask_ref, inputs_ref, weights_ref, arrived,
):
    copies = []
    for n, (far, near) in enumerate((
        (inputs_hbm, inputs_ref), (weights_hbm, weights_ref), (cotangent_hbm, cotangent_ref), (mask_hbm, mask_ref),
    )):
        copies.append(pltpu.make_async_copy(far, near, arrived.at[n]))
        copies[-1].start()
    sym[0:1] = jnp.zeros((1, 96, 128), F32)
    sym[47:48] = jnp.zeros((1, 96, 128), F32)
    sym[8:40, 8:72] = sym_ref[...].astype(F32)
    sym[1:8, 8:72] = low_ref[0:7].astype(F32)
    sym[40:47, 8:72] = high_ref[0:7].astype(F32)
    before, after = left_ref[...].astype(F32), right_ref[...].astype(F32)
    sym[:, 80:88] = before[:, :8]
    sym[:, 72:80] = after[:, :8]
    masks[:, 4:8] = jnp.zeros((4, 4, 80, 128), F32)
    masks[:, 40:44] = jnp.zeros((4, 4, 80, 128), F32)
    tiles = (own_ref.at[0], own_ref.at[1], flip_ref.at[1], flip_ref.at[2])
    for k, (lows, highs) in enumerate(((7, 0), (4, 7), (3, 4), (0, 3))):
        w, at = WIDTHS[k + 1], STARTS[k + 1]
        masks[k, 8:40, 0:64] = tiles[k][...].astype(F32)
        masks[k, 8 - w : 8, 0:64] = low_ref[at : at + w].astype(F32)
        masks[k, 40 : 40 + w, 0:64] = high_ref[at : at + w].astype(F32)
        masks[k, :, 72:80] = roll8(before[:, 8:], lows)
        masks[k, :, 64:72] = roll8(after[:, 8:], highs)

    for layer in (2, 1, 0):
        for copy in {2: copies[:2], 1: (), 0: copies[2:]}[layer]:
            copy.wait()
        d = 2**layer
        first, count = ((8, 32), (6, 36), (4, 40))[layer]
        sym[:, 0:8] = sym[:, 80:88]
        sym[:, 88:96] = sym[:, 8:16]

        def gather(f, carry):
            for v in range(3):
                patches[f, :, v * 128 : (v + 1) * 128] = sym[f, 8 + d * (v - 1) : 88 + d * (v - 1)].astype(BF)
            return carry

        lax.fori_loop(first - d, first + count + d, gather, 0, unroll=2)
        total = None
        for r in (8, 24):
            right = jnp.concatenate(
                [patches[r + d * (u - 1) : r + 16 + d * (u - 1), 0:64].reshape(1024, 384) for u in range(3)], axis=1
            )
            term = jnp.dot(inputs_ref[layer, :, (r - 8) * 64 : (r + 8) * 64], right, preferred_element_type=F32)
            total = term if total is None else total + term
        for t in range(9):
            terms_ref[layer, 8 - t] = total[:, t * 128 : (t + 1) * 128] * (1.0 / 512.0)
        if layer:
            def step(i, carry):
                f = first + size * i
                here = pl.ds(f, size)
                rows = jnp.concatenate(
                    [patches[pl.ds(f + d * (u - 1), size)].reshape(size * 80, 384) for u in range(3)], axis=1
                )
                out = jnp.dot(rows, weights_ref[layer], preferred_element_type=F32)
                ahead = masks[layer - 1, here] * out[:, :128].reshape(size, 80, 128)
                back = masks[layer + 1, here] * out[:, 128:].reshape(size, 80, 128)
                sym[here, 8:88] = sym[here, 8:88] + 0.5 * (ahead + back)
                if layer == 2:
                    change[here] = ahead[:, :64]
                else:
                    change[here] = change[here] + ahead[:, :64]
                return carry

            size = STEPS[layer]
            lax.fori_loop(0, count // size, step, 0)
        else:
            def step(i, carry):
                f = size * i
                rows = jnp.concatenate(
                    [patches[pl.ds(7 + f + u, size), 0:64].reshape(size * 64, 384) for u in range(3)], axis=1
                )
                out = jnp.dot(rows, weights_ref[0, :, :128], preferred_element_type=F32).reshape(size, 64, 128)
                here = pl.ds(f, size)
                wide = cotangent_ref[here].astype(F32) + change[pl.ds(8 + f, size)]
                gradient_ref[here] = (wide + mask_ref[here].astype(F32) * out).astype(BF)
                return carry

            size = STEPS[0]
            lax.fori_loop(0, 32 // size, step, 0)


def paired(x):
    core = lax.axis_index("core")
    half = x.shape[2] // 2
    keep = lax.dynamic_slice_in_dim(x, half * core, half, axis=2)
    send = lax.dynamic_slice_in_dim(x, half * (1 - core), half, axis=2)
    got = shift(send, core_swap())
    low = jnp.where(core == 0, keep, got)
    high = jnp.where(core == 0, got, keep)
    return with_layout_constraint(jnp.concatenate([low, high], axis=1), Layout((0, 1, 2, 3)))


def turn(direct, relayed):
    far = ((lax.axis_index("z") - lax.axis_index("y")) % 4) == 2
    arrived = with_layout_constraint(jnp.where(far, relayed, direct), Layout((0, 1, 2, 3)))
    return jnp.swapaxes(arrived, -3, -2)


def total(x):
    core = lax.axis_index("core")
    rows = x.shape[0] // 2
    x = x.reshape(2, rows, 128)
    keep = lax.dynamic_index_in_dim(x, core, 0, False)
    send = lax.dynamic_index_in_dim(x, 1 - core, 0, False).astype(BF)
    swap = core_swap()
    part = (keep + shift(send, swap).astype(F32)).astype(BF).reshape(64, rows // 64, 128)
    terms = lax.all_to_all(part, CHIPS, 0, 0, tiled=True)
    mine = jnp.sum(terms.astype(F32), axis=0).astype(BF)
    copies = jnp.broadcast_to(mine[None], terms.shape)
    whole = lax.all_to_all(copies, CHIPS, 0, 0, tiled=True).reshape(rows, 128)
    other = shift(whole, swap)
    low = jnp.where(core == 0, whole, other)
    high = jnp.where(core == 0, other, whole)
    return jnp.concatenate([low, high], axis=0).astype(F32)


def per_device(cotangent, activations, active_masks, weights):
    channels = cotangent.shape[-1]
    own = (active_masks[1:] > 0).astype(BF)
    piece = paired(jnp.concatenate([cotangent[None], own], axis=0))
    first, second = mirror_steps()
    direct = shift(piece, first)
    bottom = (active_masks[0] > 0).astype(BF)
    inputs = jnp.where(active_masks > 0, activations, jnp.zeros_like(activations))
    inputs = inputs.reshape(3, -1, channels).swapaxes(1, 2)
    kernels = weights.reshape(3, 3, 3, channels, channels)[:, ::-1, ::-1].swapaxes(3, 4)
    both = jnp.concatenate([kernels, kernels.swapaxes(1, 2)], axis=-1).reshape(3, -1, 2 * channels)
    direct, bottom, inputs, both = lax.optimization_barrier((direct, bottom, inputs, both))

    flip = turn(direct, shift(direct, second))
    tile = jax.ShapeDtypeStruct((32, 64, 128), BF)
    strip = jax.ShapeDtypeStruct((15, 64, 128), BF)
    sym, down, up = call(symmetric_kernel, "symmetric", (tile, strip, strip), cotangent, flip, own)
    low, high = shift(down, neighbour(1, 0)), shift(up, neighbour(-1, 0))
    edge = jax.ShapeDtypeStruct((48, 16, 128), BF)
    ends, starts = call(
        pack_kernel, "pack", (edge, edge), sym, own, flip, low, high, scratch=[pltpu.VMEM((2, 5, 48, 8, 128), F32)]
    )
    left, right = shift(ends, neighbour(0, 1)), shift(starts, neighbour(0, -1))
    gradient, terms = call(
        blocks_kernel, "blocks", (tile, jax.ShapeDtypeStruct((3, 9, 128, 128), F32)),
        sym, own, flip, low, high, left, right, cotangent, bottom, inputs, both,
        scratch=[
            pltpu.VMEM((48, 96, 128), F32),
            pltpu.VMEM((4, 48, 80, 128), F32),
            pltpu.VMEM((48, 80, 384), BF),
            pltpu.VMEM((48, 64, 128), F32),
            pltpu.VMEM((32, 64, 128), BF),
            pltpu.VMEM((32, 64, 128), BF),
            pltpu.VMEM((3, 128, 2048), BF),
            pltpu.VMEM((3, 1152, 256), BF),
            pltpu.SemaphoreType.DMA((4,)),
        ],
        far=4,
        flops=8 * 10**9, moved=2 * 10**7, room=60,
    )
    return gradient, total(terms.reshape(-1, channels)).reshape(terms.shape)


def solution(mesh):
    fine = Mesh(mesh.devices.reshape(SIZES), NAMES)
    rows, cols = ("y", "xh", "core"), ("z", "xl")
    in_specs = (P(rows, cols, None), P(None, rows, cols, None), P(None, rows, cols, None), P())
    out_specs = (P(rows, cols, None), P())
    return jax.shard_map(per_device, mesh=fine, in_specs=in_specs, out_specs=out_specs, check_vma=False)
```

```python
import numpy as np
import jax
import jax.numpy as jnp
from jax import lax
from jax.experimental import pallas as pl
from jax.experimental.layout import Layout, with_layout_constraint
from jax.experimental.pallas import tpu as pltpu
from jax.sharding import Mesh, PartitionSpec as P

NAMES = ("y", "xh", "core", "z", "xl")
SIZES = (4, 2, 2, 4, 2)
CHIPS = ("y", "xh", "z", "xl")
BF = jnp.bfloat16
F32 = jnp.float32


def index_grid():
    return np.arange(128).reshape(SIZES)


def neighbour(down, across):
    pairs = []
    for r in range(16):
        for c in range(8):
            if 0 <= r + down < 16 and 0 <= c + across < 8:
                pairs.append((r * 8 + c, (r + down) * 8 + c + across))
    return pairs


def mirror_steps():
    grid = index_grid()
    first, second = [], []
    for y, xh, c, z, xl in np.ndindex(*SIZES):
        source = int(grid[y, xh, c, z, xl])
        target = int(grid[z, xl, c, y, xh])
        if (z - y) % 4 == 2:
            step = 1 if c == 0 else -1
            relay = ((y + step) % 4, xl, c, (z + step) % 4, xh) if c == 0 else ((y + step) % 4, xh, c, (z + step) % 4, xl)
            first.append((source, int(grid[relay])))
            second.append((int(grid[relay]), target))
        else:
            first.append((source, target))
    return first, second


def core_swap():
    grid = index_grid()
    return [
        (int(grid[y, a, c, z, b]), int(grid[y, a, 1 - c, z, b]))
        for y, a, c, z, b in np.ndindex(*SIZES)
    ]


def shift(x, pairs):
    return lax.ppermute(x, NAMES, pairs)


WIDTHS = (7, 1, 3, 1, 3)
STARTS = (0, 7, 8, 11, 12)
STEPS = (32, 18, 20)


def roll8(x, by):
    by = by % 8
    return pltpu.roll(x, by, 1) if by else x


def call(body, name, out_shape, *args, scratch=(), flops=10**6, moved=10**6, room=8, far=0):
    return pl.pallas_call(
        body,
        out_shape=out_shape,
        in_specs=[
            pl.BlockSpec(memory_space=pltpu.SMEM if a.ndim == 1 else pltpu.VMEM if n < len(args) - far else pltpu.HBM)
            for n, a in enumerate(args)
        ],
        scratch_shapes=list(scratch),
        compiler_params=pltpu.CompilerParams(vmem_limit_bytes=room * 2**20),
        cost_estimate=pl.CostEstimate(flops=flops, bytes_accessed=moved, transcendentals=0),
        name=name,
    )(*args)


def symmetric_kernel(cotangent_ref, flip_ref, own_ref, sym_ref, down_ref, up_ref):
    wide = cotangent_ref[...].astype(F32) + flip_ref[0].astype(F32)
    sym_ref[...] = (wide * 0.5).astype(BF)
    tiles = (sym_ref, own_ref.at[0], own_ref.at[1], flip_ref.at[1], flip_ref.at[2])
    for tile, w, at in zip(tiles, WIDTHS, STARTS):
        down_ref[at : at + w] = tile[32 - w : 32]
        up_ref[at : at + w] = tile[0:w]


def pack_kernel(sym_ref, own_ref, flip_ref, low_ref, high_ref, ends_ref, starts_ref, edges):
    edges[...] = jnp.zeros_like(edges)
    tiles = (sym_ref, own_ref.at[0], own_ref.at[1], flip_ref.at[1], flip_ref.at[2])
    for k, (tile, w, at) in enumerate(zip(tiles, WIDTHS, STARTS)):
        for side, cols in ((0, slice(48, 64)), (1, slice(0, 16))):
            for rows, part in (
                (slice(8 - w, 8), low_ref[at : at + w, cols]),
                (slice(8, 40), tile[:, cols]),
                (slice(40, 40 + w), high_ref[at : at + w, cols]),
            ):
                wide = part.astype(F32)
                edges[side, k, rows] = wide[:, 8:] if side == 0 else wide[:, :8]
    place = lax.broadcasted_iota(jnp.int32, (48, 8, 128), 1)
    for side, out, moves in ((0, ends_ref, (1, 4, 5, 0)), (1, starts_ref, (0, 1, 4, 5))):
        one = [roll8(edges[side, 1 + k], by) for k, by in enumerate(moves)]
        block = jnp.where(place == 0, one[0], jnp.where(place < 4, one[1], jnp.where(place == 4, one[2], one[3])))
        out[...] = jnp.concatenate([edges[side, 0], block], axis=1).astype(BF)


def blocks_kernel(
    sym_ref, own_ref, flip_ref, low_ref, high_ref, left_ref, right_ref,
    core_ref, cotangent_hbm, mask_hbm, inputs_hbm, weights_hbm, gradient_ref, keep_ref, send_ref,
    sym, masks, patches, change, cotangent_ref, mask_ref, inputs_ref, weights_ref, arrived,
):
    copies = []
    for n, (far, near) in enumerate((
        (inputs_hbm, inputs_ref), (weights_hbm, weights_ref), (cotangent_hbm, cotangent_ref), (mask_hbm, mask_ref),
    )):
        copies.append(pltpu.make_async_copy(far, near, arrived.at[n]))
        copies[-1].start()
    sym[0:1] = jnp.zeros((1, 96, 128), F32)
    sym[47:48] = jnp.zeros((1, 96, 128), F32)
    sym[8:40, 8:72] = sym_ref[...].astype(F32)
    sym[1:8, 8:72] = low_ref[0:7].astype(F32)
    sym[40:47, 8:72] = high_ref[0:7].astype(F32)
    before, after = left_ref[...].astype(F32), right_ref[...].astype(F32)
    sym[:, 80:88] = before[:, :8]
    sym[:, 72:80] = after[:, :8]
    masks[:, 4:8] = jnp.zeros((4, 4, 80, 128), BF)
    masks[:, 40:44] = jnp.zeros((4, 4, 80, 128), BF)
    tiles = (own_ref.at[0], own_ref.at[1], flip_ref.at[1], flip_ref.at[2])
    for k, (lows, highs) in enumerate(((7, 0), (4, 7), (3, 4), (0, 3))):
        w, at = WIDTHS[k + 1], STARTS[k + 1]
        masks[k, 8:40, 0:64] = tiles[k][...]
        masks[k, 8 - w : 8, 0:64] = low_ref[at : at + w]
        masks[k, 40 : 40 + w, 0:64] = high_ref[at : at + w]
        rim = jnp.concatenate([roll8(after[:, 8:], highs), roll8(before[:, 8:], lows)], axis=1)
        masks[k, :, 64:80] = rim.astype(BF)

    for layer in (2, 1, 0):
        for copy in {2: copies[:2], 1: (), 0: copies[2:]}[layer]:
            copy.wait()
        d = 2**layer
        first, count = ((8, 32), (6, 36), (4, 40))[layer]
        sym[:, 0:8] = sym[:, 80:88]
        sym[:, 88:96] = sym[:, 8:16]

        def gather(f, carry):
            for v in range(3):
                patches[f, :, v * 128 : (v + 1) * 128] = sym[f, 8 + d * (v - 1) : 88 + d * (v - 1)].astype(BF)
            return carry

        lax.fori_loop(first - d, first + count + d, gather, 0, unroll=True)
        total = None
        for r in (8, 24):
            right = jnp.concatenate(
                [patches[r + d * (u - 1) : r + 16 + d * (u - 1), 0:64].reshape(1024, 384) for u in range(3)], axis=1
            )
            term = jnp.dot(inputs_ref[layer, :, (r - 8) * 64 : (r + 8) * 64], right, preferred_element_type=F32)
            total = term if total is None else total + term
        total = total * (1.0 / 512.0)
        lower = core_ref[0] == 0
        kept = jnp.where(lower, total[:64], total[64:])
        sent = jnp.where(lower, total[64:], total[:64]).astype(BF)
        for t in range(9):
            keep_ref[layer, 8 - t] = kept[:, t * 128 : (t + 1) * 128]
            send_ref[layer, 8 - t] = sent[:, t * 128 : (t + 1) * 128]
        if layer:
            def step(i, carry):
                f = first + size * i
                here = pl.ds(f, size)
                rows = jnp.concatenate(
                    [patches[pl.ds(f + d * (u - 1), size)].reshape(size * 80, 384) for u in range(3)], axis=1
                )
                out = jnp.dot(rows, weights_ref[layer], preferred_element_type=F32)
                ahead = masks[layer - 1, here].astype(F32) * out[:, :128].reshape(size, 80, 128)
                back = masks[layer + 1, here].astype(F32) * out[:, 128:].reshape(size, 80, 128)
                sym[here, 8:88] = sym[here, 8:88] + 0.5 * (ahead + back)
                if layer == 2:
                    change[here] = ahead[:, :64]
                else:
                    change[here] = change[here] + ahead[:, :64]
                return carry

            size = STEPS[layer]
            lax.fori_loop(0, count // size, step, 0)
        else:
            def step(i, carry):
                f = size * i
                rows = jnp.concatenate(
                    [patches[pl.ds(7 + f + u, size), 0:64].reshape(size * 64, 384) for u in range(3)], axis=1
                )
                out = jnp.dot(rows, weights_ref[0, :, :128], preferred_element_type=F32).reshape(size, 64, 128)
                here = pl.ds(f, size)
                wide = cotangent_ref[here].astype(F32) + change[pl.ds(8 + f, size)]
                gradient_ref[here] = (wide + mask_ref[here].astype(F32) * out).astype(BF)
                return carry

            size = STEPS[0]
            lax.fori_loop(0, 32 // size, step, 0)


def paired(x):
    core = lax.axis_index("core")
    half = x.shape[2] // 2
    keep = lax.dynamic_slice_in_dim(x, half * core, half, axis=2)
    send = lax.dynamic_slice_in_dim(x, half * (1 - core), half, axis=2)
    got = shift(send, core_swap())
    low = jnp.where(core == 0, keep, got)
    high = jnp.where(core == 0, got, keep)
    return with_layout_constraint(jnp.concatenate([low, high], axis=1), Layout((0, 1, 2, 3)))


def turn(direct, relayed):
    far = ((lax.axis_index("z") - lax.axis_index("y")) % 4) == 2
    arrived = with_layout_constraint(jnp.where(far, relayed, direct), Layout((0, 1, 2, 3)))
    return jnp.swapaxes(arrived, -3, -2)


def finish_kernel(core_ref, whole_ref, other_ref, out_ref):
    lower = core_ref[0] == 0
    whole, other = whole_ref[...].astype(F32), other_ref[...].astype(F32)
    out_ref[:, :64] = jnp.where(lower, whole, other)
    out_ref[:, 64:] = jnp.where(lower, other, whole)


def total(keep, send, core):
    part = (keep + shift(send, core_swap()).astype(F32)).astype(BF).reshape(64, -1, 128)
    terms = lax.all_to_all(part, CHIPS, 0, 0, tiled=True)
    mine = jnp.sum(terms.astype(F32), axis=0).astype(BF)
    copies = jnp.broadcast_to(mine[None], terms.shape)
    whole = lax.all_to_all(copies, CHIPS, 0, 0, tiled=True).reshape(keep.shape)
    other = shift(whole, core_swap())
    out = jax.ShapeDtypeStruct((keep.shape[0], 128, 128), F32)
    return call(finish_kernel, "finish", out, core, whole, other)


def per_device(cotangent, activations, active_masks, weights):
    channels = cotangent.shape[-1]
    own = (active_masks[1:] > 0).astype(BF)
    piece = paired(jnp.concatenate([cotangent[None], own], axis=0))
    first, second = mirror_steps()
    cut = piece.shape[1] // 2
    direct = shift(piece[:, :cut], first)
    direct2 = shift(piece[:, cut:], first)
    bottom = (active_masks[0] > 0).astype(BF)
    inputs = jnp.where(active_masks > 0, activations, jnp.zeros_like(activations))
    inputs = inputs.reshape(3, -1, channels).swapaxes(1, 2)
    kernels = weights.reshape(3, 3, 3, channels, channels)[:, ::-1, ::-1].swapaxes(3, 4)
    both = jnp.concatenate([kernels, kernels.swapaxes(1, 2)], axis=-1).reshape(3, -1, 2 * channels)
    direct2, bottom, inputs, both = lax.optimization_barrier((direct2, bottom, inputs, both))

    relayed = shift(direct, second)
    relayed2 = shift(direct2, second)
    flip = jnp.concatenate([turn(direct, relayed), turn(direct2, relayed2)], axis=2)
    tile = jax.ShapeDtypeStruct((32, 64, 128), BF)
    strip = jax.ShapeDtypeStruct((15, 64, 128), BF)
    sym, down, up = call(symmetric_kernel, "symmetric", (tile, strip, strip), cotangent, flip, own)
    low, high = shift(down, neighbour(1, 0)), shift(up, neighbour(-1, 0))
    edge = jax.ShapeDtypeStruct((48, 16, 128), BF)
    ends, starts = call(
        pack_kernel, "pack", (edge, edge), sym, own, flip, low, high, scratch=[pltpu.VMEM((2, 5, 48, 8, 128), F32)]
    )
    left, right = shift(ends, neighbour(0, 1)), shift(starts, neighbour(0, -1))
    core = lax.axis_index("core").astype(jnp.int32).reshape(1)
    halves = [jax.ShapeDtypeStruct((3, 9, 64, 128), kind) for kind in (F32, BF)]
    gradient, keep, send = call(
        blocks_kernel, "blocks", (tile, *halves), sym, own, flip, low, high, left, right, core, cotangent, bottom, inputs, both,
        scratch=[
            pltpu.VMEM((48, 96, 128), F32),
            pltpu.VMEM((4, 48, 80, 128), BF),
            pltpu.VMEM((48, 80, 384), BF),
            pltpu.VMEM((48, 64, 128), F32),
            pltpu.VMEM((32, 64, 128), BF),
            pltpu.VMEM((32, 64, 128), BF),
            pltpu.VMEM((3, 128, 2048), BF),
            pltpu.VMEM((3, 1152, 256), BF),
            pltpu.SemaphoreType.DMA((4,)),
        ],
        far=4,
        flops=8 * 10**9, moved=2 * 10**7, room=60,
    )
    sums = total(keep.reshape(27, 64, 128), send.reshape(27, 64, 128), core)
    return gradient, sums.reshape(3, 9, 128, 128)


def solution(mesh):
    fine = Mesh(mesh.devices.reshape(SIZES), NAMES)
    rows, cols = ("y", "xh", "core"), ("z", "xl")
    in_specs = (P(rows, cols, None), P(None, rows, cols, None), P(None, rows, cols, None), P())
    out_specs = (P(rows, cols, None), P())
    return jax.shard_map(per_device, mesh=fine, in_specs=in_specs, out_specs=out_specs, check_vma=False)
```

```python
import numpy as np
import jax
import jax.numpy as jnp
from jax import lax
from jax.experimental import pallas as pl
from jax.experimental.layout import Layout, with_layout_constraint
from jax.experimental.pallas import tpu as pltpu
from jax.sharding import Mesh, PartitionSpec as P

NAMES = ("y", "xh", "core", "z", "xl")
SIZES = (4, 2, 2, 4, 2)
CHIPS = ("y", "xh", "z", "xl")
BF = jnp.bfloat16
F32 = jnp.float32


def index_grid():
    return np.arange(128).reshape(SIZES)


def neighbour(down, across):
    pairs = []
    for r in range(16):
        for c in range(8):
            if 0 <= r + down < 16 and 0 <= c + across < 8:
                pairs.append((r * 8 + c, (r + down) * 8 + c + across))
    return pairs


def mirror_steps(other):
    grid = index_grid()
    first, second = [], []
    for y, xh, c, z, xl in np.ndindex(*SIZES):
        source = int(grid[y, xh, c, z, xl])
        target = int(grid[z, xl, 1 - c if other else c, y, xh])
        if (z - y) % 4 == 2:
            step = 1 if c == 0 else -1
            across = (xl, xh) if c == 0 else (xh, xl)
            relay = int(grid[(y + step) % 4, across[0], c, (z + step) % 4, across[1]])
            first.append((source, relay))
            second.append((relay, target))
        else:
            first.append((source, target))
    return first, second


def core_swap():
    grid = index_grid()
    return [
        (int(grid[y, a, c, z, b]), int(grid[y, a, 1 - c, z, b]))
        for y, a, c, z, b in np.ndindex(*SIZES)
    ]


def shift(x, pairs):
    return lax.ppermute(x, NAMES, pairs)


WIDTHS = (7, 1, 3, 1, 3)
STARTS = (0, 7, 8, 11, 12)
STEPS = (32, 18, 20)


def roll8(x, by):
    by = by % 8
    return pltpu.roll(x, by, 1) if by else x


def call(body, name, out_shape, *args, scratch=(), flops=10**6, moved=10**6, room=8, far=0):
    return pl.pallas_call(
        body,
        out_shape=out_shape,
        in_specs=[
            pl.BlockSpec(memory_space=pltpu.SMEM if a.ndim == 1 else pltpu.VMEM if n < len(args) - far else pltpu.HBM)
            for n, a in enumerate(args)
        ],
        scratch_shapes=list(scratch),
        compiler_params=pltpu.CompilerParams(vmem_limit_bytes=room * 2**20),
        cost_estimate=pl.CostEstimate(flops=flops, bytes_accessed=moved, transcendentals=0),
        name=name,
    )(*args)


def symmetric_kernel(cotangent_ref, flip_ref, own_ref, sym_ref, down_ref, up_ref):
    wide = cotangent_ref[...].astype(F32) + flip_ref[0].astype(F32)
    sym_ref[...] = (wide * 0.5).astype(BF)
    tiles = (sym_ref, own_ref.at[0], own_ref.at[1], flip_ref.at[1], flip_ref.at[2])
    for tile, w, at in zip(tiles, WIDTHS, STARTS):
        down_ref[at : at + w] = tile[32 - w : 32]
        up_ref[at : at + w] = tile[0:w]


def pack_kernel(sym_ref, own_ref, flip_ref, low_ref, high_ref, ends_ref, starts_ref, edges):
    edges[...] = jnp.zeros_like(edges)
    tiles = (sym_ref, own_ref.at[0], own_ref.at[1], flip_ref.at[1], flip_ref.at[2])
    for k, (tile, w, at) in enumerate(zip(tiles, WIDTHS, STARTS)):
        for side, cols in ((0, slice(48, 64)), (1, slice(0, 16))):
            for rows, part in (
                (slice(8 - w, 8), low_ref[at : at + w, cols]),
                (slice(8, 40), tile[:, cols]),
                (slice(40, 40 + w), high_ref[at : at + w, cols]),
            ):
                wide = part.astype(F32)
                edges[side, k, rows] = wide[:, 8:] if side == 0 else wide[:, :8]
    place = lax.broadcasted_iota(jnp.int32, (48, 8, 128), 1)
    for side, out, moves in ((0, ends_ref, (1, 4, 5, 0)), (1, starts_ref, (0, 1, 4, 5))):
        one = [roll8(edges[side, 1 + k], by) for k, by in enumerate(moves)]
        block = jnp.where(place == 0, one[0], jnp.where(place < 4, one[1], jnp.where(place == 4, one[2], one[3])))
        out[...] = jnp.concatenate([edges[side, 0], block], axis=1).astype(BF)


def blocks_kernel(
    sym_ref, own_ref, flip_ref, low_ref, high_ref, left_ref, right_ref,
    core_ref, cotangent_hbm, mask_hbm, inputs_hbm, weights_hbm, gradient_ref, keep_ref, send_ref,
    sym, masks, patches, change, cotangent_ref, mask_ref, inputs_ref, weights_ref, arrived,
):
    copies = []
    for n, (far, near) in enumerate((
        (inputs_hbm, inputs_ref), (weights_hbm, weights_ref), (cotangent_hbm, cotangent_ref), (mask_hbm, mask_ref),
    )):
        copies.append(pltpu.make_async_copy(far, near, arrived.at[n]))
        copies[-1].start()
    sym[0:1] = jnp.zeros((1, 96, 128), F32)
    sym[47:48] = jnp.zeros((1, 96, 128), F32)
    sym[8:40, 8:72] = sym_ref[...].astype(F32)
    sym[1:8, 8:72] = low_ref[0:7].astype(F32)
    sym[40:47, 8:72] = high_ref[0:7].astype(F32)
    before, after = left_ref[...].astype(F32), right_ref[...].astype(F32)
    sym[:, 80:88] = before[:, :8]
    sym[:, 72:80] = after[:, :8]
    masks[:, 4:8] = jnp.zeros((4, 4, 80, 128), BF)
    masks[:, 40:44] = jnp.zeros((4, 4, 80, 128), BF)
    tiles = (own_ref.at[0], own_ref.at[1], flip_ref.at[1], flip_ref.at[2])
    for k, (lows, highs) in enumerate(((7, 0), (4, 7), (3, 4), (0, 3))):
        w, at = WIDTHS[k + 1], STARTS[k + 1]
        masks[k, 8:40, 0:64] = tiles[k][...]
        masks[k, 8 - w : 8, 0:64] = low_ref[at : at + w]
        masks[k, 40 : 40 + w, 0:64] = high_ref[at : at + w]
        rim = jnp.concatenate([roll8(after[:, 8:], highs), roll8(before[:, 8:], lows)], axis=1)
        masks[k, :, 64:80] = rim.astype(BF)

    for layer in (2, 1, 0):
        for copy in {2: copies[:2], 1: (), 0: copies[2:]}[layer]:
            copy.wait()
        d = 2**layer
        first, count = ((8, 32), (6, 36), (4, 40))[layer]
        sym[:, 0:8] = sym[:, 80:88]
        sym[:, 88:96] = sym[:, 8:16]

        def gather(f, carry):
            for v in range(3):
                patches[f, :, v * 128 : (v + 1) * 128] = sym[f, 8 + d * (v - 1) : 88 + d * (v - 1)].astype(BF)
            return carry

        lax.fori_loop(first - d, first + count + d, gather, 0, unroll=True)
        total = None
        for r in (8, 24):
            right = jnp.concatenate(
                [patches[r + d * (u - 1) : r + 16 + d * (u - 1), 0:64].reshape(1024, 384) for u in range(3)], axis=1
            )
            term = jnp.dot(inputs_ref[layer, :, (r - 8) * 64 : (r + 8) * 64], right, preferred_element_type=F32)
            total = term if total is None else total + term
        total = total * (1.0 / 512.0)
        lower = core_ref[0] == 0
        kept = jnp.where(lower, total[:64], total[64:])
        sent = jnp.where(lower, total[64:], total[:64]).astype(BF)
        for t in range(9):
            keep_ref[layer, 8 - t] = kept[:, t * 128 : (t + 1) * 128]
            send_ref[layer, 8 - t] = sent[:, t * 128 : (t + 1) * 128]
        if layer:
            def step(i, carry):
                f = first + size * i
                here = pl.ds(f, size)
                rows = jnp.concatenate(
                    [patches[pl.ds(f + d * (u - 1), size)].reshape(size * 80, 384) for u in range(3)], axis=1
                )
                out = jnp.dot(rows, weights_ref[layer], preferred_element_type=F32)
                ahead = masks[layer - 1, here].astype(F32) * out[:, :128].reshape(size, 80, 128)
                back = masks[layer + 1, here].astype(F32) * out[:, 128:].reshape(size, 80, 128)
                sym[here, 8:88] = sym[here, 8:88] + 0.5 * (ahead + back)
                if layer == 2:
                    change[here] = ahead[:, :64]
                else:
                    change[here] = change[here] + ahead[:, :64]
                return carry

            size = STEPS[layer]
            lax.fori_loop(0, count // size, step, 0)
        else:
            def step(i, carry):
                f = size * i
                rows = jnp.concatenate(
                    [patches[pl.ds(7 + f + u, size), 0:64].reshape(size * 64, 384) for u in range(3)], axis=1
                )
                out = jnp.dot(rows, weights_ref[0, :, :128], preferred_element_type=F32).reshape(size, 64, 128)
                here = pl.ds(f, size)
                wide = cotangent_ref[here].astype(F32) + change[pl.ds(8 + f, size)]
                gradient_ref[here] = (wide + mask_ref[here].astype(F32) * out).astype(BF)
                return carry

            size = STEPS[0]
            lax.fori_loop(0, 32 // size, step, 0)


def turn(direct, second):
    far = ((lax.axis_index("z") - lax.axis_index("y")) % 4) == 2
    arrived = jnp.where(far, shift(direct, second), direct)
    return jnp.swapaxes(with_layout_constraint(arrived, Layout((0, 1, 2, 3))), -3, -2)


def finish_kernel(core_ref, whole_ref, other_ref, out_ref):
    lower = core_ref[0] == 0
    whole, other = whole_ref[...].astype(F32), other_ref[...].astype(F32)
    out_ref[:, :64] = jnp.where(lower, whole, other)
    out_ref[:, 64:] = jnp.where(lower, other, whole)


def total(keep, send, core):
    part = (keep + shift(send, core_swap()).astype(F32)).astype(BF).reshape(64, -1, 128)
    terms = lax.all_to_all(part, CHIPS, 0, 0, tiled=True)
    mine = jnp.sum(terms.astype(F32), axis=0).astype(BF)
    copies = jnp.broadcast_to(mine[None], terms.shape)
    whole = lax.all_to_all(copies, CHIPS, 0, 0, tiled=True).reshape(keep.shape)
    other = shift(whole, core_swap())
    out = jax.ShapeDtypeStruct((keep.shape[0], 128, 128), F32)
    return call(finish_kernel, "finish", out, core, whole, other)


def per_device(cotangent, activations, active_masks, weights):
    channels = cotangent.shape[-1]
    own = (active_masks[1:] > 0).astype(BF)
    core = lax.axis_index("core")
    stack = jnp.concatenate([cotangent[None], own], axis=0)
    half = stack.shape[2] // 2
    arriving = []
    for other, start in ((False, half * core), (True, half * (1 - core))):
        piece = with_layout_constraint(lax.dynamic_slice_in_dim(stack, start, half, axis=2), Layout((0, 1, 2, 3)))
        first, second = mirror_steps(other)
        arriving.append((shift(piece, first), second, start))
    (direct, second, start), (direct2, second2, start2) = arriving
    bottom = (active_masks[0] > 0).astype(BF)
    inputs = jnp.where(active_masks > 0, activations, jnp.zeros_like(activations))
    inputs = inputs.reshape(3, -1, channels).swapaxes(1, 2)
    kernels = weights.reshape(3, 3, 3, channels, channels)[:, ::-1, ::-1].swapaxes(3, 4)
    both = jnp.concatenate([kernels, kernels.swapaxes(1, 2)], axis=-1).reshape(3, -1, 2 * channels)
    direct2, bottom, inputs, both = lax.optimization_barrier((direct2, bottom, inputs, both))

    flip = jnp.zeros_like(stack)
    flip = lax.dynamic_update_slice_in_dim(flip, turn(direct, second), start, axis=2)
    flip = lax.dynamic_update_slice_in_dim(flip, turn(direct2, second2), start2, axis=2)
    tile = jax.ShapeDtypeStruct((32, 64, 128), BF)
    strip = jax.ShapeDtypeStruct((15, 64, 128), BF)
    sym, down, up = call(symmetric_kernel, "symmetric", (tile, strip, strip), cotangent, flip, own)
    low, high = shift(down, neighbour(1, 0)), shift(up, neighbour(-1, 0))
    edge = jax.ShapeDtypeStruct((48, 16, 128), BF)
    ends, starts = call(
        pack_kernel, "pack", (edge, edge), sym, own, flip, low, high, scratch=[pltpu.VMEM((2, 5, 48, 8, 128), F32)]
    )
    left, right = shift(ends, neighbour(0, 1)), shift(starts, neighbour(0, -1))
    core = core.astype(jnp.int32).reshape(1)
    halves = [jax.ShapeDtypeStruct((3, 9, 64, 128), kind) for kind in (F32, BF)]
    gradient, keep, send = call(
        blocks_kernel, "blocks", (tile, *halves), sym, own, flip, low, high, left, right, core, cotangent, bottom, inputs, both,
        scratch=[
            pltpu.VMEM((48, 96, 128), F32),
            pltpu.VMEM((4, 48, 80, 128), BF),
            pltpu.VMEM((48, 80, 384), BF),
            pltpu.VMEM((48, 64, 128), F32),
            pltpu.VMEM((32, 64, 128), BF),
            pltpu.VMEM((32, 64, 128), BF),
            pltpu.VMEM((3, 128, 2048), BF),
            pltpu.VMEM((3, 1152, 256), BF),
            pltpu.SemaphoreType.DMA((4,)),
        ],
        far=4,
        flops=8 * 10**9, moved=2 * 10**7, room=60,
    )
    sums = total(keep.reshape(27, 64, 128), send.reshape(27, 64, 128), core)
    return gradient, sums.reshape(3, 9, 128, 128)


def solution(mesh):
    fine = Mesh(mesh.devices.reshape(SIZES), NAMES)
    rows, cols = ("y", "xh", "core"), ("z", "xl")
    in_specs = (P(rows, cols, None), P(None, rows, cols, None), P(None, rows, cols, None), P())
    out_specs = (P(rows, cols, None), P())
    return jax.shard_map(per_device, mesh=fine, in_specs=in_specs, out_specs=out_specs, check_vma=False)
```

```python
import numpy as np
import jax
import jax.numpy as jnp
from jax import lax
from jax.experimental import pallas as pl
from jax.experimental.layout import Layout, with_layout_constraint
from jax.experimental.pallas import tpu as pltpu
from jax.sharding import Mesh, PartitionSpec as P

NAMES = ("y", "xh", "core", "z", "xl")
SIZES = (4, 2, 2, 4, 2)
CHIPS = ("y", "xh", "z", "xl")
BF = jnp.bfloat16
F32 = jnp.float32


def index_grid():
    return np.arange(128).reshape(SIZES)


def neighbour(down, across):
    pairs = []
    for r in range(16):
        for c in range(8):
            if 0 <= r + down < 16 and 0 <= c + across < 8:
                pairs.append((r * 8 + c, (r + down) * 8 + c + across))
    return pairs


def mirror_steps(other):
    grid = index_grid()
    first, second = [], []
    for y, xh, c, z, xl in np.ndindex(*SIZES):
        source = int(grid[y, xh, c, z, xl])
        target = int(grid[z, xl, 1 - c if other else c, y, xh])
        if (z - y) % 4 == 2:
            step = 1 if c == 0 else -1
            across = (xl, xh) if c == 0 else (xh, xl)
            relay = int(grid[(y + step) % 4, across[0], c, (z + step) % 4, across[1]])
            first.append((source, relay))
            second.append((relay, target))
        else:
            first.append((source, target))
    return first, second


def core_swap():
    grid = index_grid()
    return [
        (int(grid[y, a, c, z, b]), int(grid[y, a, 1 - c, z, b]))
        for y, a, c, z, b in np.ndindex(*SIZES)
    ]


def shift(x, pairs):
    return lax.ppermute(x, NAMES, pairs)


WIDTHS = (7, 1, 3, 1, 3)
STARTS = (0, 7, 8, 11, 12)
STEPS = (32, 18, 20)


def roll8(x, by):
    by = by % 8
    return pltpu.roll(x, by, 1) if by else x


def call(body, name, out_shape, *args, scratch=(), flops=10**6, moved=10**6, room=8, far=0):
    return pl.pallas_call(
        body,
        out_shape=out_shape,
        in_specs=[
            pl.BlockSpec(memory_space=pltpu.SMEM if a.ndim == 1 else pltpu.VMEM if n < len(args) - far else pltpu.HBM)
            for n, a in enumerate(args)
        ],
        scratch_shapes=list(scratch),
        compiler_params=pltpu.CompilerParams(vmem_limit_bytes=room * 2**20),
        cost_estimate=pl.CostEstimate(flops=flops, bytes_accessed=moved, transcendentals=0),
        name=name,
    )(*args)


def symmetric_kernel(cotangent_ref, flip_ref, own_ref, sym_ref, down_ref, up_ref):
    wide = cotangent_ref[...].astype(F32) + flip_ref[0].astype(F32)
    sym_ref[...] = (wide * 0.5).astype(BF)
    tiles = (sym_ref, own_ref.at[0], own_ref.at[1], flip_ref.at[1], flip_ref.at[2])
    for tile, w, at in zip(tiles, WIDTHS, STARTS):
        down_ref[at : at + w] = tile[32 - w : 32]
        up_ref[at : at + w] = tile[0:w]


def pack_kernel(sym_ref, own_ref, flip_ref, low_ref, high_ref, ends_ref, starts_ref, edges):
    edges[...] = jnp.zeros_like(edges)
    tiles = (sym_ref, own_ref.at[0], own_ref.at[1], flip_ref.at[1], flip_ref.at[2])
    for k, (tile, w, at) in enumerate(zip(tiles, WIDTHS, STARTS)):
        for side, cols in ((0, slice(48, 64)), (1, slice(0, 16))):
            for rows, part in (
                (slice(8 - w, 8), low_ref[at : at + w, cols]),
                (slice(8, 40), tile[:, cols]),
                (slice(40, 40 + w), high_ref[at : at + w, cols]),
            ):
                wide = part.astype(F32)
                edges[side, k, rows] = wide[:, 8:] if side == 0 else wide[:, :8]
    place = lax.broadcasted_iota(jnp.int32, (48, 8, 128), 1)
    for side, out, moves in ((0, ends_ref, (1, 4, 5, 0)), (1, starts_ref, (0, 1, 4, 5))):
        one = [roll8(edges[side, 1 + k], by) for k, by in enumerate(moves)]
        block = jnp.where(place == 0, one[0], jnp.where(place < 4, one[1], jnp.where(place == 4, one[2], one[3])))
        out[...] = jnp.concatenate([edges[side, 0], block], axis=1).astype(BF)


def blocks_kernel(
    sym_ref, low_ref, high_ref, left_ref, right_ref, core_ref, own_hbm, flip_hbm, cotangent_hbm, mask_hbm, inputs_hbm, weights_hbm,
    gradient_ref, keep_ref, send_ref,
    sym, masks, patches, change, cotangent_ref, mask_ref, inputs_ref, weights_ref, arrived,
):
    def fetch(n, far, near):
        copy = pltpu.make_async_copy(far, near, arrived.at[n])
        copy.start()
        return copy

    tile = (slice(8, 40), slice(0, 64))
    needed = {}
    for layer in (2, 1, 0):
        n = 4 * layer
        ahead = [fetch(n, inputs_hbm.at[layer], inputs_ref.at[layer])]
        beside = [fetch(n + 1, weights_hbm.at[layer], weights_ref.at[layer])]
        if layer:
            beside.append(fetch(n + 2, own_hbm.at[layer - 1], masks.at[(layer - 1, *tile)]))
            beside.append(fetch(n + 3, flip_hbm.at[layer], masks.at[(layer + 1, *tile)]))
        else:
            beside.append(fetch(n + 2, cotangent_hbm, cotangent_ref))
            beside.append(fetch(n + 3, mask_hbm, mask_ref))
        needed[layer] = (ahead, beside)

    sym[0:1] = jnp.zeros((1, 96, 128), F32)
    sym[47:48] = jnp.zeros((1, 96, 128), F32)
    sym[8:40, 8:72] = sym_ref[...].astype(F32)
    sym[1:8, 8:72] = low_ref[0:7].astype(F32)
    sym[40:47, 8:72] = high_ref[0:7].astype(F32)
    before, after = left_ref[...].astype(F32), right_ref[...].astype(F32)
    sym[:, 80:88] = before[:, :8]
    sym[:, 72:80] = after[:, :8]
    masks[:, 4:8] = jnp.zeros((4, 4, 80, 128), BF)
    masks[:, 40:44] = jnp.zeros((4, 4, 80, 128), BF)
    for k, (lows, highs) in enumerate(((7, 0), (4, 7), (3, 4), (0, 3))):
        w, at = WIDTHS[k + 1], STARTS[k + 1]
        masks[k, 8 - w : 8, 0:64] = low_ref[at : at + w]
        masks[k, 40 : 40 + w, 0:64] = high_ref[at : at + w]
        rim = jnp.concatenate([roll8(after[:, 8:], highs), roll8(before[:, 8:], lows)], axis=1)
        masks[k, :, 64:80] = rim.astype(BF)

    for layer in (2, 1, 0):
        d = 2**layer
        first, count = ((8, 32), (6, 36), (4, 40))[layer]
        sym[:, 0:8] = sym[:, 80:88]
        sym[:, 88:96] = sym[:, 8:16]

        def gather(f, carry):
            for v in range(3):
                patches[f, :, v * 128 : (v + 1) * 128] = sym[f, 8 + d * (v - 1) : 88 + d * (v - 1)].astype(BF)
            return carry

        lax.fori_loop(first - d, first + count + d, gather, 0, unroll=True)
        for copy in needed[layer][0]:
            copy.wait()
        total = None
        for r in (8, 24):
            right = jnp.concatenate(
                [patches[r + d * (u - 1) : r + 16 + d * (u - 1), 0:64].reshape(1024, 384) for u in range(3)], axis=1
            )
            term = jnp.dot(inputs_ref[layer, :, (r - 8) * 64 : (r + 8) * 64], right, preferred_element_type=F32)
            total = term if total is None else total + term
        total = total * (1.0 / 512.0)
        lower = core_ref[0] == 0
        kept = jnp.where(lower, total[:64], total[64:])
        sent = jnp.where(lower, total[64:], total[:64]).astype(BF)
        for t in range(9):
            keep_ref[layer, 8 - t] = kept[:, t * 128 : (t + 1) * 128]
            send_ref[layer, 8 - t] = sent[:, t * 128 : (t + 1) * 128]
        for copy in needed[layer][1]:
            copy.wait()
        if layer:
            def step(i, carry):
                f = first + size * i
                here = pl.ds(f, size)
                rows = jnp.concatenate(
                    [patches[pl.ds(f + d * (u - 1), size)].reshape(size * 80, 384) for u in range(3)], axis=1
                )
                out = jnp.dot(rows, weights_ref[layer], preferred_element_type=F32)
                ahead = masks[layer - 1, here].astype(F32) * out[:, :128].reshape(size, 80, 128)
                back = masks[layer + 1, here].astype(F32) * out[:, 128:].reshape(size, 80, 128)
                sym[here, 8:88] = sym[here, 8:88] + 0.5 * (ahead + back)
                if layer == 2:
                    change[here] = ahead[:, :64]
                else:
                    change[here] = change[here] + ahead[:, :64]
                return carry

            size = STEPS[layer]
            lax.fori_loop(0, count // size, step, 0)
        else:
            def step(i, carry):
                f = size * i
                rows = jnp.concatenate(
                    [patches[pl.ds(7 + f + u, size), 0:64].reshape(size * 64, 384) for u in range(3)], axis=1
                )
                out = jnp.dot(rows, weights_ref[0, :, :128], preferred_element_type=F32).reshape(size, 64, 128)
                here = pl.ds(f, size)
                wide = cotangent_ref[here].astype(F32) + change[pl.ds(8 + f, size)]
                gradient_ref[here] = (wide + mask_ref[here].astype(F32) * out).astype(BF)
                return carry

            size = STEPS[0]
            lax.fori_loop(0, 32 // size, step, 0)


def turn(direct, second):
    far = ((lax.axis_index("z") - lax.axis_index("y")) % 4) == 2
    arrived = jnp.where(far, shift(direct, second), direct)
    return jnp.swapaxes(arrived, -3, -2)


def finish_kernel(core_ref, whole_ref, other_ref, out_ref):
    lower = core_ref[0] == 0
    whole, other = whole_ref[...].astype(F32), other_ref[...].astype(F32)
    out_ref[:, :64] = jnp.where(lower, whole, other)
    out_ref[:, 64:] = jnp.where(lower, other, whole)


def total(keep, send, core):
    part = (keep + shift(send, core_swap()).astype(F32)).astype(BF).reshape(64, -1, 128)
    terms = lax.all_to_all(part, CHIPS, 0, 0, tiled=True)
    mine = jnp.sum(terms.astype(F32), axis=0).astype(BF)
    copies = jnp.broadcast_to(mine[None], terms.shape)
    whole = lax.all_to_all(copies, CHIPS, 0, 0, tiled=True).reshape(keep.shape)
    other = shift(whole, core_swap())
    out = jax.ShapeDtypeStruct((keep.shape[0], 128, 128), F32)
    return call(finish_kernel, "finish", out, core, whole, other)


def per_device(cotangent, activations, active_masks, weights):
    channels = cotangent.shape[-1]
    own = (active_masks[1:] > 0).astype(BF)
    core = lax.axis_index("core")
    stack = jnp.concatenate([cotangent[None], own], axis=0)
    half = stack.shape[2] // 2
    arriving = []
    for other, start in ((False, half * core), (True, half * (1 - core))):
        piece = with_layout_constraint(lax.dynamic_slice_in_dim(stack, start, half, axis=2), Layout((0, 1, 2, 3)))
        first, second = mirror_steps(other)
        arriving.append((shift(piece, first), second, start))
    (direct, second, start), (direct2, second2, start2) = arriving
    bottom = (active_masks[0] > 0).astype(BF)
    inputs = jnp.where(active_masks > 0, activations, jnp.zeros_like(activations))
    inputs = inputs.reshape(3, -1, channels).swapaxes(1, 2)
    kernels = weights.reshape(3, 3, 3, channels, channels)[:, ::-1, ::-1].swapaxes(3, 4)
    both = jnp.concatenate([kernels, kernels.swapaxes(1, 2)], axis=-1).reshape(3, -1, 2 * channels)
    direct2, bottom, inputs, both = lax.optimization_barrier((direct2, bottom, inputs, both))

    flip = jnp.zeros_like(stack)
    flip = lax.dynamic_update_slice_in_dim(flip, turn(direct, second), start, axis=2)
    flip = lax.dynamic_update_slice_in_dim(flip, turn(direct2, second2), start2, axis=2)
    tile = jax.ShapeDtypeStruct((32, 64, 128), BF)
    strip = jax.ShapeDtypeStruct((15, 64, 128), BF)
    sym, down, up = call(symmetric_kernel, "symmetric", (tile, strip, strip), cotangent, flip, own)
    low, high = shift(down, neighbour(1, 0)), shift(up, neighbour(-1, 0))
    edge = jax.ShapeDtypeStruct((48, 16, 128), BF)
    ends, starts = call(
        pack_kernel, "pack", (edge, edge), sym, own, flip, low, high, scratch=[pltpu.VMEM((2, 5, 48, 8, 128), F32)]
    )
    left, right = shift(ends, neighbour(0, 1)), shift(starts, neighbour(0, -1))
    core = core.astype(jnp.int32).reshape(1)
    halves = [jax.ShapeDtypeStruct((3, 9, 64, 128), kind) for kind in (F32, BF)]
    gradient, keep, send = call(
        blocks_kernel, "blocks", (tile, *halves), sym, low, high, left, right, core,
        own, flip, cotangent, bottom, inputs, both,
        scratch=[
            pltpu.VMEM((48, 96, 128), F32),
            pltpu.VMEM((4, 48, 80, 128), BF),
            pltpu.VMEM((48, 80, 384), BF),
            pltpu.VMEM((48, 64, 128), F32),
            pltpu.VMEM((32, 64, 128), BF),
            pltpu.VMEM((32, 64, 128), BF),
            pltpu.VMEM((3, 128, 2048), BF),
            pltpu.VMEM((3, 1152, 256), BF),
            pltpu.SemaphoreType.DMA((12,)),
        ],
        far=6,
        flops=8 * 10**9, moved=2 * 10**7, room=60,
    )
    sums = total(keep.reshape(27, 64, 128), send.reshape(27, 64, 128), core)
    return gradient, sums.reshape(3, 9, 128, 128)


def solution(mesh):
    fine = Mesh(mesh.devices.reshape(SIZES), NAMES)
    rows, cols = ("y", "xh", "core"), ("z", "xl")
    in_specs = (P(rows, cols, None), P(None, rows, cols, None), P(None, rows, cols, None), P())
    out_specs = (P(rows, cols, None), P())
    return jax.shard_map(per_device, mesh=fine, in_specs=in_specs, out_specs=out_specs, check_vma=False)
```

```python
import numpy as np
import jax
import jax.numpy as jnp
from jax import lax
from jax.experimental import pallas as pl
from jax.experimental.layout import Layout, with_layout_constraint
from jax.experimental.pallas import tpu as pltpu
from jax.sharding import Mesh, PartitionSpec as P

NAMES = ("y", "xh", "core", "z", "xl")
SIZES = (4, 2, 2, 4, 2)
CHIPS = ("y", "xh", "z", "xl")
BF = jnp.bfloat16
F32 = jnp.float32


def index_grid():
    return np.arange(128).reshape(SIZES)


def neighbour(down, across):
    pairs = []
    for r in range(16):
        for c in range(8):
            if 0 <= r + down < 16 and 0 <= c + across < 8:
                pairs.append((r * 8 + c, (r + down) * 8 + c + across))
    return pairs


def mirror_steps(other):
    grid = index_grid()
    first, second = [], []
    for y, xh, c, z, xl in np.ndindex(*SIZES):
        source = int(grid[y, xh, c, z, xl])
        target = int(grid[z, xl, 1 - c if other else c, y, xh])
        if (z - y) % 4 == 2:
            step = 1 if c == 0 else -1
            across = (xl, xh) if c == 0 else (xh, xl)
            relay = int(grid[(y + step) % 4, across[0], c, (z + step) % 4, across[1]])
            first.append((source, relay))
            second.append((relay, target))
        else:
            first.append((source, target))
    return first, second


def core_swap():
    grid = index_grid()
    return [
        (int(grid[y, a, c, z, b]), int(grid[y, a, 1 - c, z, b]))
        for y, a, c, z, b in np.ndindex(*SIZES)
    ]


def shift(x, pairs):
    return lax.ppermute(x, NAMES, pairs)


WIDTHS = (7, 1, 3, 1, 3)
STARTS = (0, 7, 8, 11, 12)
STEPS = (32, 18, 20)


def roll8(x, by):
    by = by % 8
    return pltpu.roll(x, by, 1) if by else x


def call(body, name, out_shape, *args, scratch=(), flops=10**6, moved=10**6, room=8, far=0):
    return pl.pallas_call(
        body,
        out_shape=out_shape,
        in_specs=[
            pl.BlockSpec(memory_space=pltpu.SMEM if a.ndim == 1 else pltpu.VMEM if n < len(args) - far else pltpu.HBM)
            for n, a in enumerate(args)
        ],
        scratch_shapes=list(scratch),
        compiler_params=pltpu.CompilerParams(vmem_limit_bytes=room * 2**20),
        cost_estimate=pl.CostEstimate(flops=flops, bytes_accessed=moved, transcendentals=0),
        name=name,
    )(*args)


def symmetric_kernel(cotangent_ref, flip_ref, own_ref, sym_ref, down_ref, up_ref):
    wide = cotangent_ref[...].astype(F32) + flip_ref[0].astype(F32)
    sym_ref[...] = (wide * 0.5).astype(BF)
    tiles = (sym_ref, own_ref.at[0], own_ref.at[1], flip_ref.at[1], flip_ref.at[2])
    for tile, w, at in zip(tiles, WIDTHS, STARTS):
        down_ref[at : at + w] = tile[32 - w : 32]
        up_ref[at : at + w] = tile[0:w]


def pack_kernel(sym_ref, own_ref, flip_ref, low_ref, high_ref, ends_ref, starts_ref, edges):
    edges[...] = jnp.zeros_like(edges)
    tiles = (sym_ref, own_ref.at[0], own_ref.at[1], flip_ref.at[1], flip_ref.at[2])
    for k, (tile, w, at) in enumerate(zip(tiles, WIDTHS, STARTS)):
        for side, cols in ((0, slice(48, 64)), (1, slice(0, 16))):
            for rows, part in (
                (slice(8 - w, 8), low_ref[at : at + w, cols]),
                (slice(8, 40), tile[:, cols]),
                (slice(40, 40 + w), high_ref[at : at + w, cols]),
            ):
                wide = part.astype(F32)
                edges[side, k, rows] = wide[:, 8:] if side == 0 else wide[:, :8]
    place = lax.broadcasted_iota(jnp.int32, (48, 8, 128), 1)
    for side, out, moves in ((0, ends_ref, (1, 4, 5, 0)), (1, starts_ref, (0, 1, 4, 5))):
        one = [roll8(edges[side, 1 + k], by) for k, by in enumerate(moves)]
        block = jnp.where(place == 0, one[0], jnp.where(place < 4, one[1], jnp.where(place == 4, one[2], one[3])))
        out[...] = jnp.concatenate([edges[side, 0], block], axis=1).astype(BF)


def blocks_kernel(
    sym_ref, low_ref, high_ref, left_ref, right_ref, core_ref, own_hbm, flip_hbm, cotangent_hbm, mask_hbm, inputs_hbm, weights_hbm,
    gradient_ref, keep_ref, send_ref,
    sym, masks, patches, change, cotangent_ref, mask_ref, inputs_ref, weights_ref, arrived,
):
    def fetch(n, far, near):
        copy = pltpu.make_async_copy(far, near, arrived.at[n])
        copy.start()
        return copy

    tile = (slice(8, 40), slice(0, 64))
    needed = {}
    for layer in (2, 1, 0):
        n = 4 * layer
        ahead = [fetch(n, inputs_hbm.at[layer], inputs_ref.at[layer])]
        beside = [fetch(n + 1, weights_hbm.at[layer], weights_ref.at[layer])]
        if layer:
            beside.append(fetch(n + 2, own_hbm.at[layer - 1], masks.at[(layer - 1, *tile)]))
            beside.append(fetch(n + 3, flip_hbm.at[layer], masks.at[(layer + 1, *tile)]))
        else:
            beside.append(fetch(n + 2, cotangent_hbm, cotangent_ref))
            beside.append(fetch(n + 3, mask_hbm, mask_ref))
        needed[layer] = (ahead, beside)

    sym[0:1] = jnp.zeros((1, 96, 128), F32)
    sym[47:48] = jnp.zeros((1, 96, 128), F32)
    sym[8:40, 8:72] = sym_ref[...].astype(F32)
    sym[1:8, 8:72] = low_ref[0:7].astype(F32)
    sym[40:47, 8:72] = high_ref[0:7].astype(F32)
    before, after = left_ref[...].astype(F32), right_ref[...].astype(F32)
    sym[:, 80:88] = before[:, :8]
    sym[:, 72:80] = after[:, :8]
    masks[:, 4:8] = jnp.zeros((4, 4, 80, 128), BF)
    masks[:, 40:44] = jnp.zeros((4, 4, 80, 128), BF)
    for k, (lows, highs) in enumerate(((7, 0), (4, 7), (3, 4), (0, 3))):
        w, at = WIDTHS[k + 1], STARTS[k + 1]
        masks[k, 8 - w : 8, 0:64] = low_ref[at : at + w]
        masks[k, 40 : 40 + w, 0:64] = high_ref[at : at + w]
        rim = jnp.concatenate([roll8(after[:, 8:], highs), roll8(before[:, 8:], lows)], axis=1)
        masks[k, :, 64:80] = rim.astype(BF)

    for layer in (2, 1, 0):
        d = 2**layer
        first, count = ((8, 32), (6, 36), (4, 40))[layer]
        sym[:, 0:8] = sym[:, 80:88]
        sym[:, 88:96] = sym[:, 8:16]

        def gather(f, carry):
            for v in range(3):
                patches[f, :, v * 128 : (v + 1) * 128] = sym[f, 8 + d * (v - 1) : 88 + d * (v - 1)].astype(BF)
            return carry

        lax.fori_loop(first - d, first + count + d, gather, 0, unroll=True)
        for copy in needed[layer][0]:
            copy.wait()
        total = None
        for r in (8, 24):
            right = jnp.concatenate(
                [patches[r + d * (u - 1) : r + 16 + d * (u - 1), 0:64].reshape(1024, 384) for u in range(3)], axis=1
            )
            term = jnp.dot(inputs_ref[layer, :, (r - 8) * 64 : (r + 8) * 64], right, preferred_element_type=F32)
            total = term if total is None else total + term
        total = total * (1.0 / 512.0)
        lower = core_ref[0] == 0
        kept = jnp.where(lower, total[:64], total[64:])
        sent = jnp.where(lower, total[64:], total[:64]).astype(BF)
        for t in range(9):
            keep_ref[layer, 8 - t] = kept[:, t * 128 : (t + 1) * 128]
            send_ref[layer, 8 - t] = sent[:, t * 128 : (t + 1) * 128]
        for copy in needed[layer][1]:
            copy.wait()
        if layer:
            def step(i, carry):
                f = first + size * i
                here = pl.ds(f, size)
                rows = jnp.concatenate(
                    [patches[pl.ds(f + d * (u - 1), size)].reshape(size * 80, 384) for u in range(3)], axis=1
                )
                out = jnp.dot(rows, weights_ref[layer], preferred_element_type=F32)
                ahead = masks[layer - 1, here].astype(F32) * out[:, :128].reshape(size, 80, 128)
                back = masks[layer + 1, here].astype(F32) * out[:, 128:].reshape(size, 80, 128)
                sym[here, 8:88] = sym[here, 8:88] + 0.5 * (ahead + back)
                if layer == 2:
                    change[here] = ahead[:, :64]
                else:
                    change[here] = change[here] + ahead[:, :64]
                return carry

            size = STEPS[layer]
            lax.fori_loop(0, count // size, step, 0)
        else:
            def step(i, carry):
                f = size * i
                rows = jnp.concatenate(
                    [patches[pl.ds(7 + f + u, size), 0:64].reshape(size * 64, 384) for u in range(3)], axis=1
                )
                out = jnp.dot(rows, weights_ref[0, :, :128], preferred_element_type=F32).reshape(size, 64, 128)
                here = pl.ds(f, size)
                wide = cotangent_ref[here].astype(F32) + change[pl.ds(8 + f, size)]
                gradient_ref[here] = (wide + mask_ref[here].astype(F32) * out).astype(BF)
                return carry

            size = STEPS[0]
            lax.fori_loop(0, 32 // size, step, 0)


def turn(direct, second):
    far = ((lax.axis_index("z") - lax.axis_index("y")) % 4) == 2
    arrived = jnp.where(far, shift(direct, second), direct)
    return jnp.swapaxes(arrived, -3, -2)


def finish_kernel(core_ref, whole_ref, other_ref, out_ref):
    lower = core_ref[0] == 0
    whole, other = whole_ref[...].astype(F32), other_ref[...].astype(F32)
    out_ref[:, :64] = jnp.where(lower, whole, other)
    out_ref[:, 64:] = jnp.where(lower, other, whole)


def total(keep, send, core):
    flat = (keep + shift(send, core_swap()).astype(F32)).astype(BF).reshape(-1, 128)
    count = flat.shape[0]
    part = jnp.pad(flat, ((0, 2048 - count), (0, 0))).reshape(64, 32, 128)
    terms = lax.all_to_all(part, CHIPS, 0, 0, tiled=True)
    mine = jnp.sum(terms.astype(F32), axis=0).astype(BF)
    copies = jnp.broadcast_to(mine[None], terms.shape)
    whole = lax.all_to_all(copies, CHIPS, 0, 0, tiled=True).reshape(2048, 128)[:count].reshape(keep.shape)
    other = shift(whole, core_swap())
    out = jax.ShapeDtypeStruct((keep.shape[0], 128, 128), F32)
    return call(finish_kernel, "finish", out, core, whole, other)


def per_device(cotangent, activations, active_masks, weights):
    channels = cotangent.shape[-1]
    own = (active_masks[1:] > 0).astype(BF)
    core = lax.axis_index("core")
    stack = jnp.concatenate([cotangent[None], own], axis=0)
    half = stack.shape[2] // 2
    arriving = []
    for other, start in ((False, half * core), (True, half * (1 - core))):
        piece = with_layout_constraint(lax.dynamic_slice_in_dim(stack, start, half, axis=2), Layout((0, 1, 2, 3)))
        first, second = mirror_steps(other)
        arriving.append((shift(piece, first), second, start))
    (direct, second, start), (direct2, second2, start2) = arriving
    bottom = (active_masks[0] > 0).astype(BF)
    inputs = jnp.where(active_masks > 0, activations, jnp.zeros_like(activations))
    inputs = inputs.reshape(3, -1, channels).swapaxes(1, 2)
    kernels = weights.reshape(3, 3, 3, channels, channels)[:, ::-1, ::-1].swapaxes(3, 4)
    both = jnp.concatenate([kernels, kernels.swapaxes(1, 2)], axis=-1).reshape(3, -1, 2 * channels)
    direct2, bottom, inputs, both = lax.optimization_barrier((direct2, bottom, inputs, both))

    flip = jnp.zeros_like(stack)
    flip = lax.dynamic_update_slice_in_dim(flip, turn(direct, second), start, axis=2)
    flip = lax.dynamic_update_slice_in_dim(flip, turn(direct2, second2), start2, axis=2)
    tile = jax.ShapeDtypeStruct((32, 64, 128), BF)
    strip = jax.ShapeDtypeStruct((15, 64, 128), BF)
    sym, down, up = call(symmetric_kernel, "symmetric", (tile, strip, strip), cotangent, flip, own)
    low, high = shift(down, neighbour(1, 0)), shift(up, neighbour(-1, 0))
    edge = jax.ShapeDtypeStruct((48, 16, 128), BF)
    ends, starts = call(
        pack_kernel, "pack", (edge, edge), sym, own, flip, low, high, scratch=[pltpu.VMEM((2, 5, 48, 8, 128), F32)]
    )
    left, right = shift(ends, neighbour(0, 1)), shift(starts, neighbour(0, -1))
    core = core.astype(jnp.int32).reshape(1)
    halves = [jax.ShapeDtypeStruct((3, 9, 64, 128), kind) for kind in (F32, BF)]
    gradient, keep, send = call(
        blocks_kernel, "blocks", (tile, *halves), sym, low, high, left, right, core,
        own, flip, cotangent, bottom, inputs, both,
        scratch=[
            pltpu.VMEM((48, 96, 128), F32),
            pltpu.VMEM((4, 48, 80, 128), BF),
            pltpu.VMEM((48, 80, 384), BF),
            pltpu.VMEM((48, 64, 128), F32),
            pltpu.VMEM((32, 64, 128), BF),
            pltpu.VMEM((32, 64, 128), BF),
            pltpu.VMEM((3, 128, 2048), BF),
            pltpu.VMEM((3, 1152, 256), BF),
            pltpu.SemaphoreType.DMA((12,)),
        ],
        far=6,
        flops=8 * 10**9, moved=2 * 10**7, room=42,
    )
    sums = total(keep.reshape(27, 64, 128), send.reshape(27, 64, 128), core)
    return gradient, sums.reshape(3, 9, 128, 128)


def solution(mesh):
    fine = Mesh(mesh.devices.reshape(SIZES), NAMES)
    rows, cols = ("y", "xh", "core"), ("z", "xl")
    in_specs = (P(rows, cols, None), P(None, rows, cols, None), P(None, rows, cols, None), P())
    out_specs = (P(rows, cols, None), P())
    return jax.shard_map(per_device, mesh=fine, in_specs=in_specs, out_specs=out_specs, check_vma=False)
```

```python
import numpy as np
import jax
import jax.numpy as jnp
from jax import lax
from jax.experimental import pallas as pl
from jax.experimental.layout import Layout, with_layout_constraint
from jax.experimental.pallas import tpu as pltpu
from jax.sharding import Mesh, PartitionSpec as P

NAMES = ("y", "xh", "core", "z", "xl")
SIZES = (4, 2, 2, 4, 2)
CHIPS = ("y", "xh", "z", "xl")
BF = jnp.bfloat16
F32 = jnp.float32


def index_grid():
    return np.arange(128).reshape(SIZES)


def neighbour(down, across):
    pairs = []
    for r in range(16):
        for c in range(8):
            if 0 <= r + down < 16 and 0 <= c + across < 8:
                pairs.append((r * 8 + c, (r + down) * 8 + c + across))
    return pairs


def mirror_steps(other):
    grid = index_grid()
    first, second = [], []
    for y, xh, c, z, xl in np.ndindex(*SIZES):
        source = int(grid[y, xh, c, z, xl])
        target = int(grid[z, xl, 1 - c if other else c, y, xh])
        if (z - y) % 4 == 2:
            step = 1 if c == 0 else -1
            across = (xl, xh) if c == 0 else (xh, xl)
            relay = int(grid[(y + step) % 4, across[0], c, (z + step) % 4, across[1]])
            first.append((source, relay))
            second.append((relay, target))
        else:
            first.append((source, target))
    return first, second


def core_swap():
    grid = index_grid()
    return [
        (int(grid[y, a, c, z, b]), int(grid[y, a, 1 - c, z, b]))
        for y, a, c, z, b in np.ndindex(*SIZES)
    ]


def shift(x, pairs):
    return lax.ppermute(x, NAMES, pairs)


WIDTHS = (7, 1, 3, 1, 3)
STARTS = (0, 7, 8, 11, 12)
STEPS = (32, 18, 20)


def roll8(x, by):
    by = by % 8
    return pltpu.roll(x, by, 1) if by else x


def call(body, name, out_shape, *args, scratch=(), flops=10**6, moved=10**6, room=8, far=0):
    return pl.pallas_call(
        body,
        out_shape=out_shape,
        in_specs=[
            pl.BlockSpec(memory_space=pltpu.SMEM if a.ndim == 1 else pltpu.VMEM if n < len(args) - far else pltpu.HBM)
            for n, a in enumerate(args)
        ],
        scratch_shapes=list(scratch),
        compiler_params=pltpu.CompilerParams(vmem_limit_bytes=room * 2**20),
        cost_estimate=pl.CostEstimate(flops=flops, bytes_accessed=moved, transcendentals=0),
        name=name,
    )(*args)


def symmetric_kernel(cotangent_ref, flip_ref, own_ref, sym_ref, down_ref, up_ref):
    wide = cotangent_ref[...].astype(F32) + flip_ref[0].astype(F32)
    sym_ref[...] = (wide * 0.5).astype(BF)
    tiles = (sym_ref, own_ref.at[0], own_ref.at[1], flip_ref.at[1], flip_ref.at[2])
    for tile, w, at in zip(tiles, WIDTHS, STARTS):
        down_ref[at : at + w] = tile[32 - w : 32]
        up_ref[at : at + w] = tile[0:w]


def pack_kernel(sym_ref, own_ref, flip_ref, low_ref, high_ref, ends_ref, starts_ref, edges):
    edges[...] = jnp.zeros_like(edges)
    tiles = (sym_ref, own_ref.at[0], own_ref.at[1], flip_ref.at[1], flip_ref.at[2])
    for k, (tile, w, at) in enumerate(zip(tiles, WIDTHS, STARTS)):
        for side, cols in ((0, slice(48, 64)), (1, slice(0, 16))):
            for rows, part in (
                (slice(8 - w, 8), low_ref[at : at + w, cols]),
                (slice(8, 40), tile[:, cols]),
                (slice(40, 40 + w), high_ref[at : at + w, cols]),
            ):
                wide = part.astype(F32)
                edges[side, k, rows] = wide[:, 8:] if side == 0 else wide[:, :8]
    place = lax.broadcasted_iota(jnp.int32, (48, 8, 128), 1)
    for side, out, moves in ((0, ends_ref, (1, 4, 5, 0)), (1, starts_ref, (0, 1, 4, 5))):
        one = [roll8(edges[side, 1 + k], by) for k, by in enumerate(moves)]
        block = jnp.where(place == 0, one[0], jnp.where(place < 4, one[1], jnp.where(place == 4, one[2], one[3])))
        out[...] = jnp.concatenate([edges[side, 0], block], axis=1).astype(BF)


def blocks_kernel(
    sym_ref, low_ref, high_ref, left_ref, right_ref, core_ref, own_hbm, flip_hbm, cotangent_hbm, mask_hbm, inputs_hbm, weights_hbm,
    gradient_ref, keep_ref, send_ref,
    sym, masks, patches, change, cotangent_ref, mask_ref, inputs_ref, weights_ref, arrived,
):
    def fetch(n, far, near):
        copy = pltpu.make_async_copy(far, near, arrived.at[n])
        copy.start()
        return copy

    tile = (slice(8, 40), slice(0, 64))
    needed = {}
    for layer in (2, 1, 0):
        n = 4 * layer
        ahead = [fetch(n, inputs_hbm.at[layer], inputs_ref.at[layer])]
        beside = [fetch(n + 1, weights_hbm.at[layer], weights_ref.at[layer])]
        if layer:
            beside.append(fetch(n + 2, own_hbm.at[layer - 1], masks.at[(layer - 1, *tile)]))
            beside.append(fetch(n + 3, flip_hbm.at[layer], masks.at[(layer + 1, *tile)]))
        else:
            beside.append(fetch(n + 2, cotangent_hbm, cotangent_ref))
            beside.append(fetch(n + 3, mask_hbm, mask_ref))
        needed[layer] = (ahead, beside)

    sym[0:1] = jnp.zeros((1, 96, 128), F32)
    sym[47:48] = jnp.zeros((1, 96, 128), F32)
    sym[8:40, 8:72] = sym_ref[...].astype(F32)
    sym[1:8, 8:72] = low_ref[0:7].astype(F32)
    sym[40:47, 8:72] = high_ref[0:7].astype(F32)
    before, after = left_ref[...].astype(F32), right_ref[...].astype(F32)
    sym[:, 80:88] = before[:, :8]
    sym[:, 72:80] = after[:, :8]
    masks[:, 4:8] = jnp.zeros((4, 4, 80, 128), BF)
    masks[:, 40:44] = jnp.zeros((4, 4, 80, 128), BF)
    for k, (lows, highs) in enumerate(((7, 0), (4, 7), (3, 4), (0, 3))):
        w, at = WIDTHS[k + 1], STARTS[k + 1]
        masks[k, 8 - w : 8, 0:64] = low_ref[at : at + w]
        masks[k, 40 : 40 + w, 0:64] = high_ref[at : at + w]
        rim = jnp.concatenate([roll8(after[:, 8:], highs), roll8(before[:, 8:], lows)], axis=1)
        masks[k, :, 64:80] = rim.astype(BF)

    for layer in (2, 1, 0):
        d = 2**layer
        first, count = ((8, 32), (6, 36), (4, 40))[layer]
        sym[:, 0:8] = sym[:, 80:88]
        sym[:, 88:96] = sym[:, 8:16]

        def gather(f, carry):
            for v in range(3):
                patches[f, :, v * 128 : (v + 1) * 128] = sym[f, 8 + d * (v - 1) : 88 + d * (v - 1)].astype(BF)
            return carry

        lax.fori_loop(first - d, first + count + d, gather, 0, unroll=True)
        for copy in needed[layer][0]:
            copy.wait()
        total = None
        for r in (8, 24):
            right = jnp.concatenate(
                [patches[r + d * (u - 1) : r + 16 + d * (u - 1), 0:64].reshape(1024, 384) for u in range(3)], axis=1
            )
            term = jnp.dot(inputs_ref[layer, :, (r - 8) * 64 : (r + 8) * 64], right, preferred_element_type=F32)
            total = term if total is None else total + term
        total = total * (1.0 / 512.0)
        lower = core_ref[0] == 0
        kept = jnp.where(lower, total[:64], total[64:])
        sent = jnp.where(lower, total[64:], total[:64]).astype(BF)
        for t in range(9):
            keep_ref[layer, 8 - t] = kept[:, t * 128 : (t + 1) * 128]
            send_ref[layer, 8 - t] = sent[:, t * 128 : (t + 1) * 128]
        for copy in needed[layer][1]:
            copy.wait()
        if layer:
            def step(i, carry):
                f = first + size * i
                here = pl.ds(f, size)
                rows = jnp.concatenate(
                    [patches[pl.ds(f + d * (u - 1), size)].reshape(size * 80, 384) for u in range(3)], axis=1
                )
                out = jnp.dot(rows, weights_ref[layer], preferred_element_type=F32)
                ahead = masks[layer - 1, here].astype(F32) * out[:, :128].reshape(size, 80, 128)
                back = masks[layer + 1, here].astype(F32) * out[:, 128:].reshape(size, 80, 128)
                sym[here, 8:88] = sym[here, 8:88] + 0.5 * (ahead + back)
                if layer == 2:
                    change[here] = ahead[:, :64]
                else:
                    change[here] = change[here] + ahead[:, :64]
                return carry

            size = STEPS[layer]
            lax.fori_loop(0, count // size, step, 0)
        else:
            def step(i, carry):
                f = size * i
                rows = jnp.concatenate(
                    [patches[pl.ds(7 + f + u, size), 0:64].reshape(size * 64, 384) for u in range(3)], axis=1
                )
                out = jnp.dot(rows, weights_ref[0, :, :128], preferred_element_type=F32).reshape(size, 64, 128)
                here = pl.ds(f, size)
                wide = cotangent_ref[here].astype(F32) + change[pl.ds(8 + f, size)]
                gradient_ref[here] = (wide + mask_ref[here].astype(F32) * out).astype(BF)
                return carry

            size = STEPS[0]
            lax.fori_loop(0, 32 // size, step, 0)


def turn(direct, second):
    far = ((lax.axis_index("z") - lax.axis_index("y")) % 4) == 2
    arrived = jnp.where(far, shift(direct, second), direct)
    return jnp.swapaxes(arrived, -3, -2)


def finish_kernel(core_ref, whole_ref, other_ref, out_ref):
    lower = core_ref[0] == 0
    whole, other = whole_ref[...].astype(F32), other_ref[...].astype(F32)
    out_ref[:, :64] = jnp.where(lower, whole, other)
    out_ref[:, 64:] = jnp.where(lower, other, whole)


def total(keep, send, core):
    flat = (keep + shift(send, core_swap()).astype(F32)).astype(BF).reshape(-1, 128)
    count = flat.shape[0]
    part = jnp.pad(flat, ((0, 2048 - count), (0, 0))).reshape(64, 32, 128)
    terms = lax.all_to_all(part, CHIPS, 0, 0, tiled=True)
    mine = jnp.sum(terms.astype(F32), axis=0).astype(BF)
    copies = jnp.broadcast_to(mine[None], terms.shape)
    whole = lax.all_to_all(copies, CHIPS, 0, 0, tiled=True).reshape(2048, 128)[:count].reshape(keep.shape)
    other = shift(whole, core_swap())
    out = jax.ShapeDtypeStruct((keep.shape[0], 128, 128), F32)
    return call(finish_kernel, "finish", out, core, whole, other)


def per_device(cotangent, activations, active_masks, weights):
    channels = cotangent.shape[-1]
    own = (active_masks[1:] > 0).astype(BF)
    core = lax.axis_index("core")
    stack = jnp.concatenate([cotangent[None], own], axis=0)
    half = stack.shape[2] // 2
    arriving = []
    for other, start in ((False, half * core), (True, half * (1 - core))):
        piece = with_layout_constraint(lax.dynamic_slice_in_dim(stack, start, half, axis=2), Layout((0, 1, 2, 3)))
        first, second = mirror_steps(other)
        arriving.append((shift(piece, first), second, start))
    (direct, second, start), (direct2, second2, start2) = arriving
    bottom = (active_masks[0] > 0).astype(BF)
    inputs = jnp.where(active_masks > 0, activations, jnp.zeros_like(activations))
    inputs = inputs.reshape(3, -1, channels).swapaxes(1, 2)
    kernels = weights.reshape(3, 3, 3, channels, channels)[:, ::-1, ::-1].swapaxes(3, 4)
    both = jnp.concatenate([kernels, kernels.swapaxes(1, 2)], axis=-1).reshape(3, -1, 2 * channels)
    direct2, bottom, inputs, both = lax.optimization_barrier((direct2, bottom, inputs, both))

    flip = stack
    flip = lax.dynamic_update_slice_in_dim(flip, turn(direct, second), start, axis=2)
    flip = lax.dynamic_update_slice_in_dim(flip, turn(direct2, second2), start2, axis=2)
    tile = jax.ShapeDtypeStruct((32, 64, 128), BF)
    strip = jax.ShapeDtypeStruct((15, 64, 128), BF)
    sym, down, up = call(symmetric_kernel, "symmetric", (tile, strip, strip), cotangent, flip, own)
    low, high = shift(down, neighbour(1, 0)), shift(up, neighbour(-1, 0))
    edge = jax.ShapeDtypeStruct((48, 16, 128), BF)
    ends, starts = call(
        pack_kernel, "pack", (edge, edge), sym, own, flip, low, high, scratch=[pltpu.VMEM((2, 5, 48, 8, 128), F32)]
    )
    left, right = shift(ends, neighbour(0, 1)), shift(starts, neighbour(0, -1))
    core = core.astype(jnp.int32).reshape(1)
    halves = [jax.ShapeDtypeStruct((3, 9, 64, 128), kind) for kind in (F32, BF)]
    gradient, keep, send = call(
        blocks_kernel, "blocks", (tile, *halves), sym, low, high, left, right, core,
        own, flip, cotangent, bottom, inputs, both,
        scratch=[
            pltpu.VMEM((48, 96, 128), F32),
            pltpu.VMEM((4, 48, 80, 128), BF),
            pltpu.VMEM((48, 80, 384), BF),
            pltpu.VMEM((48, 64, 128), F32),
            pltpu.VMEM((32, 64, 128), BF),
            pltpu.VMEM((32, 64, 128), BF),
            pltpu.VMEM((3, 128, 2048), BF),
            pltpu.VMEM((3, 1152, 256), BF),
            pltpu.SemaphoreType.DMA((12,)),
        ],
        far=6,
        flops=8 * 10**9, moved=2 * 10**7, room=42,
    )
    sums = total(keep.reshape(27, 64, 128), send.reshape(27, 64, 128), core)
    return gradient, sums.reshape(3, 9, 128, 128)


def solution(mesh):
    fine = Mesh(mesh.devices.reshape(SIZES), NAMES)
    rows, cols = ("y", "xh", "core"), ("z", "xl")
    in_specs = (P(rows, cols, None), P(None, rows, cols, None), P(None, rows, cols, None), P())
    out_specs = (P(rows, cols, None), P())
    return jax.shard_map(per_device, mesh=fine, in_specs=in_specs, out_specs=out_specs, check_vma=False)
```
